512 devices in a mesh: rep: 16 (over y, core), vol: 32 (over z, x).
Axes of the slice: x: 4, y: 8, z: 8, core: 2. Of those that a mesh axis runs over, the one named last changes fastest.
Arguments:
- positions: float32 [131072, 2, 24], P(('rep', 'vol')), may hold values from -1 to 1
- spacing: float32 [131072, 2, 8], P(('rep', 'vol')), may hold values from 0.05 to 0.5
- volume_ids: int32 [131072, 2], P(('rep', 'vol')), may hold values from 0 to 127, all different within a row; in each aligned block of 256 rows (0 to 255, 256 to 511, ...) at most 8 rows name the same one
- target: float32 [3, 131072], P(None, ('rep', 'vol')), may hold values from 0 to 1
- w_in: bfloat16 [128, 64, 256], P('vol'), may hold values from -0.75 to 0.75
- w_hidden: bfloat16 [128, 256, 256], P('vol'), may hold values from -0.375 to 0.375
- w_head: bfloat16 [128, 4, 256], P('vol'), may hold values from -0.375 to 0.375
Outputs:
- rendered: float32 [3, 131072], P(None, ('rep', 'vol'))
- grad_in: float32 [128, 64, 256], P('vol', None, 'rep')
- grad_hidden: float32 [128, 256, 256], P('vol', 'rep')
- grad_head: float32 [128, 4, 256], P('vol', None, 'rep')
The draws below stay inside these ranges and needn't reach their ends.
Inputs may be any that keep to these rules, and one draw needn't show every extreme that they name: `volume_ids`: the 2 entries of a ray are different sub-volumes, nearest first. Among the 256 rays of one device no sub-volume is named more than 8 times, and in some device's rays one is named exactly 8 times.
All inputs are finite; a program needn't handle non-finite values.
Results may differ from the reference program's by a relative error of at most 0.012.
Values may be sent and summed in bfloat16 or wider, within the bound.
A program may use at most 64 MiB of HBM per device.

```python
import math
import jax
import jax.numpy as jnp
import numpy as np
from jax import lax

FREQS = 10
ENC = 64
WIDTH = 256
TOP = 2
SAMPLES = 8
RAYS_DEV = 256
VOLUMES = 128
RAYS = 131072
CAP = 8
N_REP = 16
N_VOL = 32


def levels(rng, shape, shards, smallest, top_value):
    loudness = 1.0
    for position, parts in shards:
        draws = jax.random.uniform(jax.random.fold_in(jax.random.fold_in(rng, 6), position), (parts,), jnp.float32, smallest / len(shards), top_value / len(shards))
        loudness = loudness * jnp.repeat(jnp.exp(draws), shape[position] // parts).reshape((-1,) + (1,) * (len(shape) - 1 - position))
    return loudness


def shared_out(own_key, own, number, rows, count, top, bound, skew):
    sequence = jax.random.permutation(own_key, count)
    heavy_load, ordinary = load_shares(count, rows * top, bound, skew, True), load_shares(count, rows * top, bound, skew, False)
    places = jnp.arange(count)

    def named(sizes, offset_by):
        used = int((sizes > 0).sum())
        fixed = max(1, used // 4)
        passed = fixed + (places - fixed + offset_by * (used - fixed)) % max(1, count - fixed)
        return jnp.zeros((count,), jnp.int32).at[sequence[jnp.where(places < fixed, places, passed)]].set(jnp.asarray(sizes, jnp.int32))

    sizes = jnp.where(number % 4 == 0, named(heavy_load, number // 4), named(ordinary, number - number // 4 - 1))
    mixed = jax.random.permutation(jax.random.fold_in(own, 3), count)
    giver, receiver = mixed[0:count // 2 * 2:2], mixed[1:count // 2 * 2:2]
    margin = jnp.minimum(sizes[giver] - 1, bound - sizes[receiver]) // 2
    margin = jnp.where((giver == sequence[0]) | (receiver == sequence[0]) | (sizes[receiver] == 0), 0, jnp.maximum(margin, 0))
    passed = jax.random.randint(jax.random.fold_in(own, 4), (count // 2,), 0, 1 << 20) % (margin + 1)
    sizes = sizes.at[giver].add(-passed).at[receiver].add(passed)
    labels = jnp.searchsorted(jnp.cumsum(sizes), jnp.arange(rows * top), side="right").astype(jnp.int32)
    table = labels.reshape(top, rows).T
    table = table[jax.random.permutation(jax.random.fold_in(own, 1), rows)]
    offset_by = jax.random.randint(jax.random.fold_in(own, 2), (rows, 1), 0, top)
    return jnp.take_along_axis(table, (jnp.arange(top)[None, :] + offset_by) % top, axis=1)


def load_shares(amount, total, bound, lean, full):
    portions = [(1 << 20) // math.isqrt(grade ** lean) + 1 for grade in range(1, amount + 1)]
    largest = bound if full else min(bound, max(-(-total // amount), total * portions[0] // sum(portions)))
    least = 1 if total - largest >= amount - 1 else 0
    given, surplus = [largest] + [least] * (amount - 1), total - largest - least * (amount - 1)
    while surplus > 0:
        candidates = [i for i in range(1, amount) if given[i] < largest] or [i for i in range(1, amount) if given[i] < bound]
        whole, remaining = sum([portions[i] for i in candidates]), surplus
        for i in candidates:
            extra = min(bound - given[i], max(1, remaining * portions[i] // whole), surplus)
            given[i] = given[i] + extra
            surplus = surplus - extra
    return np.array(given)


def noise(stream_key, shape, deviation, limit, cuts=(), held_as=jnp.bfloat16):
    entries = deviation * jax.random.normal(stream_key, shape, jnp.float32)
    if cuts:
        entries = entries * levels(stream_key, shape, cuts, -0.22, 0.18)
    return jnp.clip(entries, -limit, limit).astype(held_as)


def setup_inputs(seed: int = 0) -> dict:
    key_list = jax.random.split(jax.random.key(seed), 8)
    positions = jnp.clip(jax.random.uniform(key_list[0], (RAYS, TOP, 3 * SAMPLES), jnp.float32, -1.0, 1.0) * levels(key_list[0], (RAYS, TOP, 3 * SAMPLES), ((0, 512),), -0.4, 0.0), -1.0, 1.0)
    spacing = jnp.clip(jnp.exp(math.log(0.5) - 2.3025851 * jax.random.uniform(key_list[1], (RAYS, TOP, SAMPLES), jnp.float32) ** levels(key_list[1], (RAYS, TOP, SAMPLES), ((0, 512),), -0.2, 0.2)), 0.05, 0.5)
    volume_ids_keys = jax.random.split(jax.random.fold_in(key_list[2], 1), RAYS // RAYS_DEV)
    volume_ids_turns = jax.random.permutation(jax.random.fold_in(key_list[2], 3), RAYS // RAYS_DEV)
    volume_ids = jax.vmap(lambda own, number: shared_out(jax.random.fold_in(key_list[2], 2), own, number, RAYS_DEV, VOLUMES, TOP, CAP, 2))(volume_ids_keys, volume_ids_turns).reshape((RAYS, TOP))
    target = jnp.clip(1.0 * jax.random.uniform(key_list[3], (3, RAYS), jnp.float32) ** levels(key_list[3], (3, RAYS), ((1, 512),), -0.2, 0.2), 0.0, 1.0)
    w_in = noise(key_list[4], (VOLUMES, ENC, WIDTH), ENC ** -0.5, 0.75, ((0, 32),))
    w_hidden = noise(key_list[5], (VOLUMES, WIDTH, WIDTH), WIDTH ** -0.5, 0.375, ((0, 32),))
    w_head = noise(key_list[6], (VOLUMES, 4, WIDTH), WIDTH ** -0.5, 0.375, ((0, 32),))
    return {"positions": positions, "spacing": spacing, "volume_ids": volume_ids, "target": target, "w_in": w_in, "w_hidden": w_hidden, "w_head": w_head}


def encode(points):
    coords = jnp.swapaxes(points, -1, -2)
    scales = (2.0 ** jnp.arange(FREQS)).astype(coords.dtype) * math.pi
    angles = (coords[..., None] * scales).reshape(coords.shape[:-1] + (3 * FREQS,))
    unit = jnp.ones(coords.shape[:-1] + (1,), coords.dtype)
    return jnp.concatenate([jnp.sin(angles), jnp.cos(angles), coords, unit], axis=-1)

def silu_slope(pre_act):
    gate = jax.nn.sigmoid(pre_act)
    return gate * (1.0 + pre_act * (1.0 - gate))

def product(left, right):
    return jnp.dot(left.astype(jnp.float32), right.astype(jnp.float32), preferred_element_type=jnp.float32)

def forward(rows, w_first, w_mid, w_last):
    pre_one = product(rows, w_first)
    act_one = jax.nn.silu(pre_one).astype(jnp.bfloat16)
    pre_two = product(act_one, w_mid)
    act_two = jax.nn.silu(pre_two).astype(jnp.bfloat16)
    raw_out = product(act_two, w_last.T)
    return (pre_one, act_one, pre_two, act_two, raw_out)

def activate(raw_out):
    return jnp.concatenate([jax.nn.sigmoid(raw_out[:, :3]), jax.nn.softplus(raw_out[:, 3:])], axis=1)

def backward(rows, cotangent, w_first, w_mid, w_last):
    pre_one, act_one, pre_two, act_two, raw_out = forward(rows, w_first, w_mid, w_last)
    gate = jax.nn.sigmoid(raw_out)
    slope = jnp.concatenate([gate[:, :3] * (1.0 - gate[:, :3]), gate[:, 3:]], axis=1)
    cot_raw = (cotangent * slope).astype(jnp.bfloat16)
    d_last = product(cot_raw.T, act_two)
    cot_two = (product(cot_raw, w_last) * silu_slope(pre_two)).astype(jnp.bfloat16)
    d_mid = product(act_one.T, cot_two)
    cot_one = (product(cot_two, w_mid.T) * silu_slope(pre_one)).astype(jnp.bfloat16)
    d_first = product(rows.T, cot_one)
    return (d_first, d_mid, d_last)

def slots_of(volume_ids, volume_count, capacity):
    flat_ids = volume_ids.reshape(-1)
    table = (flat_ids[:, None] == jnp.arange(volume_count, dtype=jnp.int32)[None, :]).astype(jnp.int32)
    earlier = jnp.cumsum(table, axis=0) - table
    return flat_ids * capacity + lax.optimization_barrier(jnp.sum(earlier * table, axis=1))

def render(radiance, spacing):
    tau = radiance[..., 3] * spacing
    alpha = 1.0 - jnp.exp(-tau)
    before = jnp.cumsum(tau, axis=-1) - tau
    share = jnp.exp(-before) * alpha
    seg_color = lax.optimization_barrier(jnp.sum(share[..., None] * radiance[..., :3], axis=-2))
    passing = jnp.exp(-lax.optimization_barrier(jnp.sum(tau, axis=-1)))
    color = seg_color[:, 0]
    carried = passing[:, 0]
    for segment in range(1, passing.shape[1]):
        color = color + carried[:, None] * seg_color[:, segment]
        carried = carried * passing[:, segment]
    return color.T

def reference(positions, spacing, volume_ids, target, w_in, w_hidden, w_head):
    group_pos = positions.reshape(N_REP, N_VOL, RAYS_DEV * TOP, 3, SAMPLES)
    group_gap = spacing.reshape(N_REP, N_VOL, RAYS_DEV, TOP, SAMPLES)
    group_ids = volume_ids.reshape(N_REP, N_VOL, RAYS_DEV, TOP)
    group_tgt = jnp.transpose(target.reshape(3, N_REP, N_VOL, RAYS_DEV), (1, 2, 0, 3))
    row_count = N_VOL * CAP * SAMPLES

    def one_group(totals, pieces):
        points, gaps, chosen_ids, wanted = pieces
        places = jax.vmap(lambda chosen: slots_of(chosen, VOLUMES, CAP))(chosen_ids)
        feats = encode(points).astype(jnp.bfloat16).reshape(N_VOL, RAYS_DEV * TOP, SAMPLES * ENC)
        empty_feat = jnp.zeros((VOLUMES * CAP, SAMPLES * ENC), jnp.bfloat16)
        buffers = jax.vmap(lambda spots, values: empty_feat.at[spots].set(values))(places, feats)
        rows = jnp.swapaxes(buffers.reshape(N_VOL, VOLUMES, CAP * SAMPLES, ENC), 0, 1).reshape(VOLUMES, row_count, ENC)
        radiance = lax.map(lambda item: activate(forward(*item)[4]), (rows, w_in, w_hidden, w_head))
        returned = jnp.swapaxes(radiance.reshape(VOLUMES, N_VOL, CAP * SAMPLES * 4), 0, 1)
        returned = returned.reshape(N_VOL, VOLUMES * CAP, SAMPLES, 4)
        per_ray = jax.vmap(lambda stored, spots: stored[spots])(returned, places)
        per_ray = per_ray.reshape(N_VOL, RAYS_DEV, TOP, SAMPLES, 4)
        color, pull = jax.vjp(lambda values: jax.vmap(render)(values, gaps), per_ray)
        cot_ray, = pull((color - wanted) / N_REP)
        empty_cot = jnp.zeros((VOLUMES * CAP, SAMPLES * 4), cot_ray.dtype)
        cot_flat = cot_ray.reshape(N_VOL, RAYS_DEV * TOP, SAMPLES * 4)
        cot_buffers = jax.vmap(lambda spots, values: empty_cot.at[spots].set(values))(places, cot_flat)
        cot_rows = jnp.swapaxes(cot_buffers.reshape(N_VOL, VOLUMES, CAP * SAMPLES * 4), 0, 1)
        cot_rows = cot_rows.reshape(VOLUMES, row_count, 4)
        partial_grads = lax.map(lambda item: backward(*item), (rows, cot_rows, w_in, w_hidden, w_head))
        totals = tuple((total + piece for total, piece in zip(totals, partial_grads)))
        return (totals, color)
    start = (jnp.zeros(w_in.shape, jnp.float32), jnp.zeros(w_hidden.shape, jnp.float32), jnp.zeros(w_head.shape, jnp.float32))
    totals, colors = lax.scan(one_group, start, (group_pos, group_gap, group_ids, group_tgt))
    rendered = jnp.transpose(colors, (2, 0, 1, 3)).reshape(3, N_REP * N_VOL * RAYS_DEV)
    return (rendered, totals[0], totals[1], totals[2])
```

```python
import functools
import math

import jax
import jax.numpy as jnp
from jax import lax
from jax.experimental import pallas as pl
from jax.experimental.pallas import tpu as pltpu
from jax.sharding import PartitionSpec as P

FREQS = 10
ENC = 64
WIDTH = 256
SAMPLES = 8
CAP = 8
HELD = 4
VALS = 4 * SAMPLES
PACK = 384
HALF = FREQS // 2
MESH = pl.DeviceIdType.MESH
BF16 = jnp.bfloat16
F32 = jnp.float32


def dot(left, right):
    return jnp.dot(left, right, preferred_element_type=F32)


def dot_nt(left, right):
    return lax.dot_general(left, right, (((1,), (1,)), ((), ())), preferred_element_type=F32)


def split3(x, axis):
    high = x.astype(BF16)
    rest = x - high.astype(F32)
    mid = rest.astype(BF16)
    low = (rest - mid.astype(F32)).astype(BF16)
    return jnp.concatenate([high, mid, low], axis=axis)


def sine_cosine(turns):
    x = turns * (math.pi / 2)
    y = x * x
    sin = jnp.full_like(y, 1.0 / math.factorial(13))
    for k in (11, 9, 7, 5, 3, 1):
        sin = (1.0 / math.factorial(k)) - y * sin
    sin = sin * x
    cos = jnp.full_like(y, 1.0 / math.factorial(12))
    for k in (10, 8, 6, 4, 2, 0):
        cos = (1.0 / math.factorial(k)) - y * cos
    return 2.0 * sin * cos, 1.0 - 2.0 * sin * sin


def sigmoid(x):
    return 1.0 / (1.0 + jnp.exp(-x))


def softplus(x):
    e = jnp.exp(-jnp.abs(x))
    small = e * (1.0 - e * (0.5 - e * (1.0 / 3.0)))
    return jnp.maximum(x, 0.0) + jnp.where(e < 1e-2, small, jnp.log(1.0 + e))


def one_hot(rows, row):
    spots = lax.broadcasted_iota(jnp.int32, (rows, row.shape[1]), 0)
    return jnp.where(spots == row, 1.0, 0.0)


def kernel(
    n_rep, n_vol, rays,
    pos, gap, ids, target, w_in, w_hidden, w_head,
    out_color, out_in, out_hidden, out_head,
    send_a, recv_a, send_b, recv_b, send_c, recv_c,
    table, feats, enc, act_one, act_two, slope_one, slope_two,
    raw_s, gap_s, cot_f, cot_two_s, cot_one_s, turn, table_t,
    w_in_t, w_hidden_t, w_head_p, w_head_t,
    part, pair_in, block_out, block_in, own_block,
    sem, pair_sem, block_sem,
):
    me_r, me_v = lax.axis_index("rep"), lax.axis_index("vol")
    n_y = n_rep // 2
    me_y, me_c = me_r // 2, lax.rem(me_r, 2)
    lanes = n_vol * CAP
    segs = 2 * rays
    volumes = n_vol * HELD
    rows = WIDTH // n_rep

    def vol_peer(k):
        return lax.rem(me_v + k, n_vol)

    def rep_peer(k):
        return lax.rem(me_y + k, n_y) * 2 + me_c

    sibling = me_y * 2 + 1 - me_c

    barrier = pltpu.get_barrier_semaphore()

    def greet_vol(k, carry):
        pl.semaphore_signal(barrier, inc=1, device_id=(me_r, vol_peer(k)), device_id_type=MESH)
        return carry

    def greet_rep(k, carry):
        pl.semaphore_signal(barrier, inc=1, device_id=(rep_peer(k), me_v), device_id_type=MESH)
        return carry

    lax.fori_loop(1, n_vol, greet_vol, 0)
    lax.fori_loop(1, n_y, greet_rep, 0)
    pl.semaphore_signal(barrier, inc=1, device_id=(sibling, me_v), device_id_type=MESH)

    id_row = jnp.concatenate([ids[0:1, :], ids[1:2, :]], axis=1)
    hot = one_hot(volumes, id_row)
    before = jnp.where(
        lax.broadcasted_iota(jnp.int32, (rays, rays), 0)
        < lax.broadcasted_iota(jnp.int32, (rays, rays), 1),
        1.0,
        0.0,
    ).astype(BF16)
    hot_0, hot_1 = hot[:, :rays], hot[:, rays:]
    earlier_0 = dot(hot_0.astype(BF16), before)
    earlier_1 = dot(hot_1.astype(BF16), before) + jnp.sum(hot_0, axis=1, keepdims=True)
    rank = jnp.concatenate(
        [
            jnp.sum(earlier_0 * hot_0, axis=0, keepdims=True),
            jnp.sum(earlier_1 * hot_1, axis=0, keepdims=True),
        ],
        axis=1,
    ).astype(jnp.int32)
    owner = lax.shift_right_logical(id_row, 2)
    held = lax.bitwise_and(id_row, 3)
    place_hot = one_hot(lanes, owner * CAP + rank).astype(BF16)
    vals = jnp.concatenate(
        [
            jnp.concatenate([pos[0], gap[0]], axis=0),
            jnp.concatenate([pos[1], gap[1]], axis=0),
        ],
        axis=1,
    )
    spread = jnp.concatenate([jnp.where(held == v, vals, 0.0) for v in range(HELD)], axis=0)
    moved = dot_nt(place_hot, split3(spread, 0))
    moved = (moved[:, 0:128] + moved[:, 128:256]) + moved[:, 256:384]
    send_a[...] = moved.reshape(n_vol, CAP, 128)
    recv_a[me_v] = send_a[me_v]
    pl.semaphore_wait(barrier, n_vol - 1 + n_y)

    def exchange(source, landing, number):
        def start(k, carry):
            peer = vol_peer(k)
            pltpu.make_async_remote_copy(
                src_ref=source.at[peer],
                dst_ref=landing.at[me_v],
                send_sem=sem.at[2 * number],
                recv_sem=sem.at[2 * number + 1],
                device_id=(me_r, peer),
                device_id_type=MESH,
            ).start()
            return carry

        lax.fori_loop(1, n_vol, start, 0)

    def await_all(buffer, which):
        span = buffer.at[pl.ds(0, n_vol - 1)]
        pltpu.make_async_copy(span, span, sem.at[which]).wait()

    exchange(send_a, recv_a, 0)

    cot_f[...] = jnp.zeros_like(cot_f)
    turn[...] = jnp.zeros_like(turn)
    w_head_p[...] = jnp.zeros_like(w_head_p)

    def turn_weights(v, carry):
        w_in_t[v] = w_in[v].astype(F32).T.astype(BF16)
        w_hidden_t[v] = w_hidden[v].astype(F32).T.astype(BF16)
        head = jnp.concatenate([w_head[v].astype(F32), jnp.zeros((124, WIDTH), F32)], axis=0)
        w_head_p[v] = head[0:16].astype(BF16)
        w_head_t[v] = head.T[:, 0:16].astype(BF16)
        return carry

    lax.fori_loop(0, HELD, turn_weights, 0)

    await_all(recv_a, 1)
    table[...] = recv_a[...].reshape(lanes, 128).T

    blocks, block = feats.shape[0], feats.shape[2]

    def put(at, values):
        for b in range(blocks):
            feats[b, at : at + values.shape[0], :] = values[:, b * block : (b + 1) * block]

    def forward(v, carry):
        base = pl.multiple_of(v * VALS, VALS)
        points = table[pl.ds(base, 24), :]
        gaps = table[pl.ds(base + 24, 8), :]
        wide = points * (2.0**HALF)
        wide = wide - 2.0 * jnp.floor(wide * 0.5 + 0.5)
        sin_lo, cos_lo = sine_cosine(points)
        sin_hi, cos_hi = sine_cosine(wide)
        for f in range(HALF):
            for offset, sin, cos in ((f, sin_lo, cos_lo), (HALF + f, sin_hi, cos_hi)):
                for c in range(3):
                    at = c * FREQS + offset
                    put(at * 8, sin[c * 8 : c * 8 + 8])
                    put((30 + at) * 8, cos[c * 8 : c * 8 + 8])
            sin_lo, cos_lo = 2.0 * sin_lo * cos_lo, 1.0 - 2.0 * sin_lo * sin_lo
            sin_hi, cos_hi = 2.0 * sin_hi * cos_hi, 1.0 - 2.0 * sin_hi * sin_hi
        put(480, points)
        put(504, jnp.ones((8, lanes), F32))
        for i in range(SAMPLES):
            span = slice(i * lanes, (i + 1) * lanes)
            features = jnp.concatenate(
                [feats[b, pl.ds(i, ENC, stride=8), :] for b in range(blocks)], axis=1
            ).astype(BF16)
            enc[v, :, span] = features
            half = 0.5 * dot(w_in_t[v], features)
            act = (half + half * jnp.tanh(half)).astype(BF16)
            act_one[v, :, span] = act
            half = 0.5 * dot(w_hidden_t[v], act)
            act = (half + half * jnp.tanh(half)).astype(BF16)
            act_two[v, :, span] = act
            raw = dot(w_head_p[v], act)
            for c in range(4):
                raw_s[c, i, pl.ds(v, 1), :] = raw[c : c + 1]
            gap_s[i, pl.ds(v, 1), :] = gaps[i : i + 1]
        return carry

    lax.fori_loop(0, HELD, forward, 0)

    shade = [[sigmoid(raw_s[c, i]) for i in range(SAMPLES)] for c in range(3)]
    dense_slope, spans, share, clear = [], [], [], []
    depth = jnp.zeros((HELD, lanes), F32)
    through = jnp.ones((HELD, lanes), F32)
    color = [jnp.zeros((HELD, lanes), F32) for _ in range(3)]
    for i in range(SAMPLES):
        raw = raw_s[3, i]
        spacing = gap_s[i]
        tau = softplus(raw) * spacing
        depth = depth + tau
        share.append(through * (1.0 - jnp.exp(-tau)))
        through = jnp.exp(-depth)
        clear.append(through)
        dense_slope.append(sigmoid(raw))
        spans.append(spacing)
        color = [color[c] + share[i] * shade[c][i] for c in range(3)]

    turn[0:16, :] = jnp.concatenate(color + [through], axis=0)
    flipped = turn[...].T
    table_t[...] = flipped
    row_b = jnp.zeros((n_vol, 128), F32)
    for j in range(CAP):
        piece = table_t[pl.ds(j, n_vol, stride=CAP), :]
        row_b = row_b + (piece if j == 0 else pltpu.roll(piece, 16 * j, 1))
    send_b[...] = row_b.reshape(n_vol, 1, 128)
    recv_b[me_v] = send_b[me_v]
    exchange(send_b, recv_b, 1)

    def slopes(v, carry):
        for i in range(SAMPLES):
            span = slice(i * lanes, (i + 1) * lanes)
            for w_t, before_s, after_s, slope_s in (
                (w_in_t, enc, act_one, slope_one),
                (w_hidden_t, act_one, act_two, slope_two),
            ):
                pre = dot(w_t[v], before_s[v, :, span])
                gate = 0.5 + 0.5 * jnp.tanh(0.5 * pre)
                slope_s[v, :, span] = (gate + pre * gate * (1.0 - gate)).astype(BF16)
        return carry

    lax.fori_loop(0, HELD // 2, slopes, 0)
    await_all(recv_b, 3)

    owner_hot = one_hot(n_vol, owner).astype(BF16)
    arrived = recv_b[...].reshape(n_vol, 128)
    arrived = jnp.concatenate([arrived, jnp.zeros((128 - n_vol, 128), F32)], axis=0)
    arrived_t = arrived.T[:, 0:n_vol]
    found = dot(split3(arrived_t, 1), jnp.concatenate([owner_hot] * 3, axis=0))
    spot = lax.broadcasted_iota(jnp.int32, (128, segs), 0)
    mine = lax.bitwise_and(spot, 0x73) == rank * 16 + held
    found = jnp.where(mine, found, 0.0)
    total = found[0:16]
    for j in range(1, CAP):
        total = total + found[16 * j : 16 * j + 16]
    per_seg = [jnp.sum(total[4 * c : 4 * c + 4], axis=0, keepdims=True) for c in range(4)]
    carried = per_seg[3][:, :rays]
    behind = jnp.zeros((1, rays), F32)
    cots = []
    for c in range(3):
        near, far = per_seg[c][:, :rays], per_seg[c][:, rays:]
        value = near + carried * far
        out_color[c : c + 1, :] = value
        slope = (value - target[c : c + 1, :]) * (1.0 / n_rep)
        behind = behind + slope * far
        cots.append(jnp.concatenate([slope, carried * slope], axis=1))
    cots.append(jnp.concatenate([behind, jnp.zeros((1, rays), F32)], axis=1))
    cots = jnp.concatenate([jnp.broadcast_to(x, (4, segs)) for x in cots], axis=0)
    cots = jnp.where(mine, jnp.concatenate([cots] * CAP, axis=0), 0.0)
    row_c = dot_nt(owner_hot, split3(cots, 0))
    row_c = (row_c[:, 0:128] + row_c[:, 128:256]) + row_c[:, 256:384]
    send_c[...] = row_c.reshape(n_vol, 1, 128)
    recv_c[me_v] = send_c[me_v]
    exchange(send_c, recv_c, 2)

    lax.fori_loop(HELD // 2, HELD, slopes, 0)
    await_all(recv_c, 5)

    row_c = recv_c[...].reshape(n_vol, 128)
    for j in range(CAP):
        piece = row_c if j == 0 else pltpu.roll(row_c, 128 - 16 * j, 1)
        table_t[pl.ds(j, n_vol, stride=CAP), :] = piece
    cots = table_t[...].T[0:16]
    cot_color = [cots[4 * c : 4 * c + 4] for c in range(3)]
    later = through * cots[12:16]
    for i in reversed(range(SAMPLES)):
        pull = sum(cot_color[c] * shade[c][i] for c in range(3))
        cot_raw = [
            cot_color[c] * share[i] * (shade[c][i] * (1.0 - shade[c][i])) for c in range(3)
        ]
        cot_raw.append((clear[i] * pull - later) * spans[i] * dense_slope[i])
        later = later + share[i] * pull
        for c in range(4):
            for v in range(HELD):
                cot_f[v, c : c + 1, i * lanes : (i + 1) * lanes] = cot_raw[c][v : v + 1]

    def pair_copy(v):
        return pltpu.make_async_remote_copy(
            src_ref=part.at[v, 1 - me_c],
            dst_ref=pair_in.at[v],
            send_sem=pair_sem.at[0, v],
            recv_sem=pair_sem.at[1, v],
            device_id=(sibling, me_v),
            device_id_type=MESH,
        )

    def pass_on(v):
        pair_copy(v).wait()
        both = part[v, me_c] + pair_in[v]
        block_out[v] = both.astype(BF16)
        own_block[...] = both
        pair_in[v, 0] = own_block[me_y]
        block_in[v, me_y] = jnp.zeros((rows, PACK), BF16)

        def start(k, carry):
            y = lax.rem(me_y + k, n_y)
            pltpu.make_async_remote_copy(
                src_ref=block_out.at[v, y],
                dst_ref=block_in.at[v, me_y],
                send_sem=block_sem.at[0, v],
                recv_sem=block_sem.at[1, v],
                device_id=(y * 2 + me_c, me_v),
                device_id_type=MESH,
            ).start()
            return carry

        lax.fori_loop(1, n_y, start, 0)

    def backward(v, carry):
        for i in range(SAMPLES):
            span = slice(i * lanes, (i + 1) * lanes)
            cot_raw = cot_f[v, :, span].astype(BF16)
            cot = dot(w_head_t[v], cot_raw) * slope_two[v, :, span].astype(F32)
            cot = cot.astype(BF16)
            cot_two_s[:, span] = cot
            cot = dot(w_hidden[v], cot) * slope_one[v, :, span].astype(F32)
            cot_one_s[:, span] = cot.astype(BF16)
        d_mid = dot_nt(act_one[v], cot_two_s[...])
        d_first = dot_nt(cot_one_s[...], enc[v])
        d_last = dot_nt(act_two[v], cot_f[v].astype(BF16))
        side = jnp.concatenate([d_first, d_last, jnp.zeros((WIDTH, 48), F32)], axis=1)
        for r in range(n_rep):
            part[v, r % 2, r // 2, :, 0:WIDTH] = d_mid[r * rows : (r + 1) * rows]
            part[v, r % 2, r // 2, :, WIDTH:PACK] = side[r * rows : (r + 1) * rows]
        pair_copy(v).start()

        @pl.when(v > 0)
        def _():
            pass_on(v - 1)

        return carry

    lax.fori_loop(0, HELD, backward, 0)
    pass_on(HELD - 1)

    heads = []
    for v in range(HELD):
        span = block_in.at[v, pl.ds(0, n_y - 1)]
        pltpu.make_async_copy(span, span, block_sem.at[1, v]).wait()
        whole = pair_in[v, 0]
        for y in range(n_y):
            whole = whole + block_in[v, y].astype(F32)
        out_hidden[v] = whole[:, 0:WIDTH]
        out_in[v] = whole[:, WIDTH : WIDTH + ENC]
        heads.append(whole[:, WIDTH:PACK])
    heads.append(jnp.zeros((max(128 - HELD * rows, 0), 128), F32))
    heads = jnp.concatenate(heads, axis=0).T
    for v in range(HELD):
        out_head[v] = heads[ENC : ENC + 4, v * rows : (v + 1) * rows]

    for number, buffer in ((0, send_a), (1, send_b), (2, send_c)):
        await_all(buffer, 2 * number)
    for v in range(HELD):
        span = block_out.at[v, pl.ds(0, n_y - 1)]
        pltpu.make_async_copy(span, span, block_sem.at[0, v]).wait()


def solution(mesh):
    n_rep, n_vol = mesh.shape["rep"], mesh.shape["vol"]

    def local(positions, spacing, volume_ids, target, w_in, w_hidden, w_head):
        rays = volume_ids.shape[0]
        lanes = n_vol * CAP
        wide = SAMPLES * lanes
        rows = WIDTH // n_rep
        n_y = n_rep // 2
        vmem = pl.BlockSpec(memory_space=pltpu.VMEM)
        outs = pl.pallas_call(
            functools.partial(kernel, n_rep, n_vol, rays),
            out_shape=(
                jax.ShapeDtypeStruct((3, rays), F32),
                jax.ShapeDtypeStruct((HELD, rows, ENC), F32),
                jax.ShapeDtypeStruct((HELD, rows, WIDTH), F32),
                jax.ShapeDtypeStruct((HELD, 4, rows), F32),
            ),
            in_specs=[vmem] * 7,
            out_specs=[vmem] * 4,
            scratch_shapes=[
                pltpu.VMEM((n_vol, CAP, 128), F32),
                pltpu.VMEM((n_vol, CAP, 128), F32),
                pltpu.VMEM((n_vol, 1, 128), F32),
                pltpu.VMEM((n_vol, 1, 128), F32),
                pltpu.VMEM((n_vol, 1, 128), F32),
                pltpu.VMEM((n_vol, 1, 128), F32),
                pltpu.VMEM((128, lanes), F32),
                pltpu.VMEM((pl.cdiv(lanes, 128), ENC * 8, min(lanes, 128)), F32),
                pltpu.VMEM((HELD, ENC, wide), BF16),
                pltpu.VMEM((HELD, WIDTH, wide), BF16),
                pltpu.VMEM((HELD, WIDTH, wide), BF16),
                pltpu.VMEM((HELD, WIDTH, wide), BF16),
                pltpu.VMEM((HELD, WIDTH, wide), BF16),
                pltpu.VMEM((4, SAMPLES, HELD, lanes), F32),
                pltpu.VMEM((SAMPLES, HELD, lanes), F32),
                pltpu.VMEM((HELD, 16, wide), F32),
                pltpu.VMEM((WIDTH, wide), BF16),
                pltpu.VMEM((WIDTH, wide), BF16),
                pltpu.VMEM((128, lanes), F32),
                pltpu.VMEM((lanes, 128), F32),
                pltpu.VMEM((HELD, WIDTH, ENC), BF16),
                pltpu.VMEM((HELD, WIDTH, WIDTH), BF16),
                pltpu.VMEM((HELD, 16, WIDTH), BF16),
                pltpu.VMEM((HELD, WIDTH, 16), BF16),
                pltpu.VMEM((HELD, 2, n_y, rows, PACK), F32),
                pltpu.VMEM((HELD, n_y, rows, PACK), F32),
                pltpu.VMEM((HELD, n_y, rows, PACK), BF16),
                pltpu.VMEM((HELD, n_y, rows, PACK), BF16),
                pltpu.VMEM((n_y, rows, PACK), F32),
                pltpu.SemaphoreType.DMA((6,)),
                pltpu.SemaphoreType.DMA((2, HELD)),
                pltpu.SemaphoreType.DMA((2, HELD)),
            ],
            compiler_params=pltpu.CompilerParams(
                collective_id=0, has_side_effects=True, vmem_limit_bytes=56 * 1024 * 1024
            ),
        )(
            jnp.transpose(positions, (1, 2, 0)),
            jnp.transpose(spacing, (1, 2, 0)),
            volume_ids.T,
            target,
            w_in,
            w_hidden,
            w_head,
        )
        color, grad_in, grad_hidden, grad_head = outs
        return color, jnp.swapaxes(grad_in, 1, 2), grad_hidden, grad_head

    return jax.shard_map(
        local,
        mesh=mesh,
        in_specs=(
            P(("rep", "vol"), None, None),
            P(("rep", "vol"), None, None),
            P(("rep", "vol"), None),
            P(None, ("rep", "vol")),
            P("vol", None, None),
            P("vol", None, None),
            P("vol", None, None),
        ),
        out_specs=(
            P(None, ("rep", "vol")),
            P("vol", None, "rep"),
            P("vol", "rep", None),
            P("vol", None, "rep"),
        ),
        check_vma=False,
    )
```

```python
import functools
import math

import jax
import jax.numpy as jnp
from jax import lax
from jax.experimental import pallas as pl
from jax.experimental.pallas import tpu as pltpu
from jax.sharding import PartitionSpec as P

FREQS = 10
ENC = 64
WIDTH = 256
SAMPLES = 8
CAP = 8
HELD = 4
VALS = 4 * SAMPLES
PACK = 384
HALF = FREQS // 2
MESH = pl.DeviceIdType.MESH
BF16 = jnp.bfloat16
F32 = jnp.float32


def dot(left, right):
    return jnp.dot(left, right, preferred_element_type=F32)


def dot_nt(left, right):
    return lax.dot_general(left, right, (((1,), (1,)), ((), ())), preferred_element_type=F32)


def split3(x, axis):
    high = x.astype(BF16)
    rest = x - high.astype(F32)
    mid = rest.astype(BF16)
    low = (rest - mid.astype(F32)).astype(BF16)
    return jnp.concatenate([high, mid, low], axis=axis)


def sine_cosine(turns):
    x = turns * (math.pi / 2)
    y = x * x
    sin = jnp.full_like(y, 1.0 / math.factorial(13))
    for k in (11, 9, 7, 5, 3, 1):
        sin = (1.0 / math.factorial(k)) - y * sin
    sin = sin * x
    cos = jnp.full_like(y, 1.0 / math.factorial(12))
    for k in (10, 8, 6, 4, 2, 0):
        cos = (1.0 / math.factorial(k)) - y * cos
    return 2.0 * sin * cos, 1.0 - 2.0 * sin * sin


def sigmoid(x):
    return 1.0 / (1.0 + jnp.exp(-x))


def softplus(x):
    e = jnp.exp(-jnp.abs(x))
    small = e * (1.0 - e * (0.5 - e * (1.0 / 3.0)))
    return jnp.maximum(x, 0.0) + jnp.where(e < 1e-2, small, jnp.log(1.0 + e))


def one_hot(rows, row):
    spots = lax.broadcasted_iota(jnp.int32, (rows, row.shape[1]), 0)
    return jnp.where(spots == row, 1.0, 0.0)


def kernel(
    n_rep, n_vol, rays,
    pos_h, gap_h, ids_h, target_h, w_in_h, w_hidden_h, w_head_h,
    out_color, out_in, out_hidden, out_head,
    send_a, recv_a, send_b, recv_b, send_c, recv_c,
    table, feats, enc, act_one, act_two, slope_one, slope_two,
    raw_s, gap_s, cot_f, cot_two_s, cot_one_s, turn, table_t,
    w_in_t, w_hidden_t, w_head_p, w_head_w,
    part, pair_in, block_out, block_in, own_block,
    pos, gap, ids, target, w_in, w_hidden, w_head,
    sem, pair_sem, block_sem, load_sem,
):
    me_r, me_v = lax.axis_index("rep"), lax.axis_index("vol")
    n_y = n_rep // 2
    me_y, me_c = me_r // 2, lax.rem(me_r, 2)
    lanes = n_vol * CAP
    segs = 2 * rays
    volumes = n_vol * HELD
    rows = WIDTH // n_rep

    n_z, n_x = n_vol // 4, 4
    me_z, me_x = me_v // n_x, lax.rem(me_v, n_x)

    def far_first(k, n):
        half = (k + 1) // 2
        return n // 2 + jnp.where(lax.rem(k, 2) == 0, half, -half)

    def vol_peer(k):
        z = lax.rem(me_z + far_first(k // n_x, n_z), n_z)
        x = lax.rem(me_x + far_first(lax.rem(k, n_x), n_x), n_x)
        return z * n_x + x

    def y_peer(k):
        return lax.rem(me_y + far_first(k, n_y), n_y)

    sibling = me_y * 2 + 1 - me_c
    blocks, block = feats.shape[0], feats.shape[2]

    loads = [
        pltpu.make_async_copy(source, place, load_sem.at[number])
        for number, (source, place) in enumerate(
            (
                (ids_h, ids), (pos_h, pos), (gap_h, gap), (w_in_h, w_in),
                (w_hidden_h, w_hidden), (w_head_h, w_head), (target_h, target),
            )
        )
    ]
    barrier = pltpu.get_barrier_semaphore()

    def greet_vol(k, carry):
        pl.semaphore_signal(barrier, inc=1, device_id=(me_r, vol_peer(k)), device_id_type=MESH)
        return carry

    def greet_rep(k, carry):
        pl.semaphore_signal(barrier, inc=1, device_id=(y_peer(k) * 2 + me_c, me_v), device_id_type=MESH)
        return carry

    lax.fori_loop(0, n_vol - 1, greet_vol, 0)
    lax.fori_loop(0, n_y - 1, greet_rep, 0)
    pl.semaphore_signal(barrier, inc=1, device_id=(sibling, me_v), device_id_type=MESH)

    for load in loads:
        load.start()
    loads[0].wait()

    id_row = jnp.concatenate([ids[0:1, :], ids[1:2, :]], axis=1)
    hot = one_hot(volumes, id_row)
    before = jnp.where(
        lax.broadcasted_iota(jnp.int32, (rays, rays), 0)
        < lax.broadcasted_iota(jnp.int32, (rays, rays), 1),
        1.0,
        0.0,
    ).astype(BF16)
    hot_0, hot_1 = hot[:, :rays], hot[:, rays:]
    earlier_0 = dot(hot_0.astype(BF16), before)
    earlier_1 = dot(hot_1.astype(BF16), before) + jnp.sum(hot_0, axis=1, keepdims=True)
    rank = jnp.concatenate(
        [
            jnp.sum(earlier_0 * hot_0, axis=0, keepdims=True),
            jnp.sum(earlier_1 * hot_1, axis=0, keepdims=True),
        ],
        axis=1,
    ).astype(jnp.int32)
    owner = lax.shift_right_logical(id_row, 2)
    held = lax.bitwise_and(id_row, 3)
    place_hot = one_hot(lanes, owner * CAP + rank).astype(BF16)
    loads[1].wait()
    loads[2].wait()
    vals = jnp.concatenate(
        [
            jnp.concatenate([pos[0], gap[0]], axis=0),
            jnp.concatenate([pos[1], gap[1]], axis=0),
        ],
        axis=1,
    )
    spread = jnp.concatenate([jnp.where(held == v, vals, 0.0) for v in range(HELD)], axis=0)
    moved = dot_nt(place_hot, split3(spread, 0))
    moved = (moved[:, 0:128] + moved[:, 128:256]) + moved[:, 256:384]
    send_a[...] = moved.reshape(n_vol, CAP, 128)
    recv_a[me_v] = send_a[me_v]
    pl.semaphore_wait(barrier, n_vol - 1 + n_y)

    def exchange(source, landing, number):
        def start(k, carry):
            peer = vol_peer(k)
            pltpu.make_async_remote_copy(
                src_ref=source.at[peer],
                dst_ref=landing.at[me_v],
                send_sem=sem.at[2 * number],
                recv_sem=sem.at[2 * number + 1],
                device_id=(me_r, peer),
                device_id_type=MESH,
            ).start()
            return carry

        lax.fori_loop(0, n_vol - 1, start, 0)

    def await_all(buffer, which):
        span = buffer.at[pl.ds(0, n_vol - 1)]
        pltpu.make_async_copy(span, span, sem.at[which]).wait()

    exchange(send_a, recv_a, 0)

    cot_f[...] = jnp.zeros_like(cot_f)
    turn[...] = jnp.zeros_like(turn)
    w_head_p[...] = jnp.zeros_like(w_head_p)

    for load in loads[3:]:
        load.wait()

    def turn_weights(v, carry):
        w_in_t[v] = w_in[v].astype(F32).T.astype(BF16)
        w_hidden_t[v] = w_hidden[v].astype(F32).T.astype(BF16)
        head = jnp.concatenate([w_head[v].astype(F32), jnp.zeros((124, WIDTH), F32)], axis=0)
        w_head_p[v] = head[0:16].astype(BF16)
        head_t = head.T
        for c in range(4):
            w_head_w[v, c] = jnp.broadcast_to(head_t[:, c : c + 1], (WIDTH, block))
        return carry

    lax.fori_loop(0, HELD, turn_weights, 0)

    await_all(recv_a, 1)
    table[...] = recv_a[...].reshape(lanes, 128).T

    def put(at, values):
        for b in range(blocks):
            feats[b, at : at + values.shape[0], :] = values[:, b * block : (b + 1) * block]

    def forward(v, carry):
        base = pl.multiple_of(v * VALS, VALS)
        points = table[pl.ds(base, 24), :]
        gaps = table[pl.ds(base + 24, 8), :]
        wide = points * (2.0**HALF)
        wide = wide - 2.0 * jnp.floor(wide * 0.5 + 0.5)
        sin_lo, cos_lo = sine_cosine(points)
        sin_hi, cos_hi = sine_cosine(wide)
        for f in range(HALF):
            for offset, sin, cos in ((f, sin_lo, cos_lo), (HALF + f, sin_hi, cos_hi)):
                for c in range(3):
                    at = c * FREQS + offset
                    put(at * 8, sin[c * 8 : c * 8 + 8])
                    put((30 + at) * 8, cos[c * 8 : c * 8 + 8])
            sin_lo, cos_lo = 2.0 * sin_lo * cos_lo, 1.0 - 2.0 * sin_lo * sin_lo
            sin_hi, cos_hi = 2.0 * sin_hi * cos_hi, 1.0 - 2.0 * sin_hi * sin_hi
        put(480, points)
        put(504, jnp.ones((8, lanes), F32))
        for i in range(SAMPLES):
            span = slice(i * lanes, (i + 1) * lanes)
            features = jnp.concatenate(
                [feats[b, pl.ds(i, ENC, stride=8), :] for b in range(blocks)], axis=1
            ).astype(BF16)
            enc[v, :, span] = features
            half = 0.5 * dot(w_in_t[v], features)
            act = (half + half * jnp.tanh(half)).astype(BF16)
            act_one[v, :, span] = act
            half = 0.5 * dot(w_hidden_t[v], act)
            act = (half + half * jnp.tanh(half)).astype(BF16)
            act_two[v, :, span] = act
            gap_s[i, pl.ds(v, 1), :] = gaps[i : i + 1]
        for i in range(SAMPLES):
            raw = dot(w_head_p[v], act_two[v, :, i * lanes : (i + 1) * lanes])
            for c in range(4):
                raw_s[c, i, pl.ds(v, 1), :] = raw[c : c + 1]
        return carry

    lax.fori_loop(0, HELD, forward, 0)

    shade = [[sigmoid(raw_s[c, i]) for i in range(SAMPLES)] for c in range(3)]
    dense_slope, spans, share, clear = [], [], [], []
    depth = jnp.zeros((HELD, lanes), F32)
    through = jnp.ones((HELD, lanes), F32)
    color = [jnp.zeros((HELD, lanes), F32) for _ in range(3)]
    for i in range(SAMPLES):
        raw = raw_s[3, i]
        spacing = gap_s[i]
        tau = softplus(raw) * spacing
        depth = depth + tau
        share.append(through * (1.0 - jnp.exp(-tau)))
        through = jnp.exp(-depth)
        clear.append(through)
        dense_slope.append(sigmoid(raw))
        spans.append(spacing)
        color = [color[c] + share[i] * shade[c][i] for c in range(3)]

    turn[0:16, :] = jnp.concatenate(color + [through], axis=0)
    flipped = turn[...].T
    table_t[...] = flipped
    row_b = jnp.zeros((n_vol, 128), F32)
    for j in range(CAP):
        piece = table_t[pl.ds(j, n_vol, stride=CAP), :]
        row_b = row_b + (piece if j == 0 else pltpu.roll(piece, 16 * j, 1))
    send_b[...] = row_b.reshape(n_vol, 1, 128)
    recv_b[me_v] = send_b[me_v]
    exchange(send_b, recv_b, 1)

    def slopes(v, carry):
        for i in range(SAMPLES):
            span = slice(i * lanes, (i + 1) * lanes)
            for w_t, before_s, after_s, slope_s in (
                (w_in_t, enc, act_one, slope_one),
                (w_hidden_t, act_one, act_two, slope_two),
            ):
                pre = dot(w_t[v], before_s[v, :, span])
                gate = 0.5 + 0.5 * jnp.tanh(0.5 * pre)
                slope_s[v, :, span] = gate + pre * gate * (1.0 - gate)
        return carry

    lax.fori_loop(0, HELD // 2, slopes, 0)
    await_all(recv_b, 3)

    owner_hot = one_hot(n_vol, owner).astype(BF16)
    arrived = recv_b[...].reshape(n_vol, 128)
    arrived = jnp.concatenate([arrived, jnp.zeros((128 - n_vol, 128), F32)], axis=0)
    arrived_t = arrived.T[:, 0:n_vol]
    found = dot(split3(arrived_t, 1), jnp.concatenate([owner_hot] * 3, axis=0))
    spot = lax.broadcasted_iota(jnp.int32, (128, segs), 0)
    mine = lax.bitwise_and(spot, 0x73) == rank * 16 + held
    found = jnp.where(mine, found, 0.0)
    total = found[0:16]
    for j in range(1, CAP):
        total = total + found[16 * j : 16 * j + 16]
    per_seg = [jnp.sum(total[4 * c : 4 * c + 4], axis=0, keepdims=True) for c in range(4)]
    carried = per_seg[3][:, :rays]
    behind = jnp.zeros((1, rays), F32)
    cots = []
    for c in range(3):
        near, far = per_seg[c][:, :rays], per_seg[c][:, rays:]
        value = near + carried * far
        out_color[c : c + 1, :] = value
        slope = (value - target[c : c + 1, :]) * (1.0 / n_rep)
        behind = behind + slope * far
        cots.append(jnp.concatenate([slope, carried * slope], axis=1))
    cots.append(jnp.concatenate([behind, jnp.zeros((1, rays), F32)], axis=1))
    cots = jnp.concatenate([jnp.broadcast_to(x, (4, segs)) for x in cots], axis=0)
    cots = jnp.where(mine, jnp.concatenate([cots] * CAP, axis=0), 0.0)
    row_c = dot_nt(owner_hot, split3(cots, 0))
    row_c = (row_c[:, 0:128] + row_c[:, 128:256]) + row_c[:, 256:384]
    send_c[...] = row_c.reshape(n_vol, 1, 128)
    recv_c[me_v] = send_c[me_v]
    exchange(send_c, recv_c, 2)

    lax.fori_loop(HELD // 2, HELD, slopes, 0)
    await_all(recv_c, 5)

    row_c = recv_c[...].reshape(n_vol, 128)
    for j in range(CAP):
        piece = row_c if j == 0 else pltpu.roll(row_c, 128 - 16 * j, 1)
        table_t[pl.ds(j, n_vol, stride=CAP), :] = piece
    cots = table_t[...].T[0:16]
    cot_color = [cots[4 * c : 4 * c + 4] for c in range(3)]
    later = through * cots[12:16]
    for i in reversed(range(SAMPLES)):
        pull = sum(cot_color[c] * shade[c][i] for c in range(3))
        cot_raw = [
            cot_color[c] * share[i] * (shade[c][i] * (1.0 - shade[c][i])) for c in range(3)
        ]
        cot_raw.append((clear[i] * pull - later) * spans[i] * dense_slope[i])
        later = later + share[i] * pull
        for c in range(4):
            for v in range(HELD):
                cot_f[v, c : c + 1, i * lanes : (i + 1) * lanes] = cot_raw[c][v : v + 1]

    def pair_copy(v):
        return pltpu.make_async_remote_copy(
            src_ref=part.at[v, 1 - me_c],
            dst_ref=pair_in.at[v],
            send_sem=pair_sem.at[0, v],
            recv_sem=pair_sem.at[1, v],
            device_id=(sibling, me_v),
            device_id_type=MESH,
        )

    def pass_on(v):
        pair_copy(v).wait()
        both = part[v, me_c] + pair_in[v]
        block_out[v] = both.astype(BF16)
        own_block[...] = both
        pair_in[v, 0] = own_block[me_y]
        block_in[v, me_y] = jnp.zeros((rows, PACK), BF16)

        def start(k, carry):
            y = y_peer(k)
            pltpu.make_async_remote_copy(
                src_ref=block_out.at[v, y],
                dst_ref=block_in.at[v, me_y],
                send_sem=block_sem.at[0, v],
                recv_sem=block_sem.at[1, v],
                device_id=(y * 2 + me_c, me_v),
                device_id_type=MESH,
            ).start()
            return carry

        lax.fori_loop(0, n_y - 1, start, 0)

    def backward(v, carry):
        for i in range(SAMPLES):
            span = slice(i * lanes, (i + 1) * lanes)
            cot_raw = cot_f[v, 0:4, span].astype(BF16).astype(F32)
            cot = sum(
                cot_raw[c : c + 1] * jnp.concatenate([w_head_w[v, c]] * blocks, axis=1)
                for c in range(4)
            )
            cot = cot * slope_two[v, :, span]
            cot = cot.astype(BF16)
            cot_two_s[:, span] = cot
            cot = dot(w_hidden[v], cot) * slope_one[v, :, span]
            cot_one_s[:, span] = cot.astype(BF16)
        d_mid = dot_nt(act_one[v], cot_two_s[...])
        d_first = dot_nt(cot_one_s[...], enc[v])
        d_last = dot_nt(cot_f[v].astype(BF16), act_two[v])
        d_last = jnp.concatenate([d_last, jnp.zeros((112, WIDTH), F32)], axis=0).T[:, 0:64]
        side = jnp.concatenate([d_first, d_last], axis=1)
        for r in range(n_rep):
            part[v, r % 2, r // 2, :, 0:WIDTH] = d_mid[r * rows : (r + 1) * rows]
            part[v, r % 2, r // 2, :, WIDTH:PACK] = side[r * rows : (r + 1) * rows]
        pair_copy(v).start()

        @pl.when(v > 0)
        def _():
            pass_on(v - 1)

        return carry

    lax.fori_loop(0, HELD, backward, 0)
    pass_on(HELD - 1)

    heads = []
    for v in range(HELD):
        span = block_in.at[v, pl.ds(0, n_y - 1)]
        pltpu.make_async_copy(span, span, block_sem.at[1, v]).wait()
        whole = pair_in[v, 0]
        for y in range(n_y):
            whole = whole + block_in[v, y].astype(F32)
        out_hidden[v] = whole[:, 0:WIDTH]
        out_in[v] = whole[:, WIDTH : WIDTH + ENC]
        heads.append(whole[:, WIDTH:PACK])
    heads.append(jnp.zeros((max(128 - HELD * rows, 0), 128), F32))
    heads = jnp.concatenate(heads, axis=0).T
    for v in range(HELD):
        out_head[v] = heads[ENC : ENC + 4, v * rows : (v + 1) * rows]

    for number, buffer in ((0, send_a), (1, send_b), (2, send_c)):
        await_all(buffer, 2 * number)
    for v in range(HELD):
        span = block_out.at[v, pl.ds(0, n_y - 1)]
        pltpu.make_async_copy(span, span, block_sem.at[0, v]).wait()


def hand_over(*refs):
    for source, result in zip(refs[:4], refs[4:]):
        result[...] = source[...]


def solution(mesh):
    n_rep, n_vol = mesh.shape["rep"], mesh.shape["vol"]

    def local(positions, spacing, volume_ids, target, w_in, w_hidden, w_head):
        rays = volume_ids.shape[0]
        lanes = n_vol * CAP
        wide = SAMPLES * lanes
        rows = WIDTH // n_rep
        n_y = n_rep // 2
        vmem = pl.BlockSpec(memory_space=pltpu.VMEM)
        shapes = (
            jax.ShapeDtypeStruct((3, rays), F32),
            jax.ShapeDtypeStruct((HELD, rows, ENC), F32),
            jax.ShapeDtypeStruct((HELD, rows, WIDTH), F32),
            jax.ShapeDtypeStruct((HELD, 4, rows), F32),
        )
        outs = pl.pallas_call(
            functools.partial(kernel, n_rep, n_vol, rays),
            out_shape=shapes,
            in_specs=[pl.BlockSpec(memory_space=pl.ANY)] * 7,
            out_specs=[vmem] * 4,
            scratch_shapes=[
                pltpu.VMEM((n_vol, CAP, 128), F32),
                pltpu.VMEM((n_vol, CAP, 128), F32),
                pltpu.VMEM((n_vol, 1, 128), F32),
                pltpu.VMEM((n_vol, 1, 128), F32),
                pltpu.VMEM((n_vol, 1, 128), F32),
                pltpu.VMEM((n_vol, 1, 128), F32),
                pltpu.VMEM((128, lanes), F32),
                pltpu.VMEM((pl.cdiv(lanes, 128), ENC * 8, min(lanes, 128)), F32),
                pltpu.VMEM((HELD, ENC, wide), BF16),
                pltpu.VMEM((HELD, WIDTH, wide), BF16),
                pltpu.VMEM((HELD, WIDTH, wide), BF16),
                pltpu.VMEM((HELD, WIDTH, wide), F32),
                pltpu.VMEM((HELD, WIDTH, wide), F32),
                pltpu.VMEM((4, SAMPLES, HELD, lanes), F32),
                pltpu.VMEM((SAMPLES, HELD, lanes), F32),
                pltpu.VMEM((HELD, 16, wide), F32),
                pltpu.VMEM((WIDTH, wide), BF16),
                pltpu.VMEM((WIDTH, wide), BF16),
                pltpu.VMEM((128, lanes), F32),
                pltpu.VMEM((lanes, 128), F32),
                pltpu.VMEM((HELD, WIDTH, ENC), BF16),
                pltpu.VMEM((HELD, WIDTH, WIDTH), BF16),
                pltpu.VMEM((HELD, 16, WIDTH), BF16),
                pltpu.VMEM((HELD, 4, WIDTH, min(lanes, 128)), F32),
                pltpu.VMEM((HELD, 2, n_y, rows, PACK), F32),
                pltpu.VMEM((HELD, n_y, rows, PACK), F32),
                pltpu.VMEM((HELD, n_y, rows, PACK), BF16),
                pltpu.VMEM((HELD, n_y, rows, PACK), BF16),
                pltpu.VMEM((n_y, rows, PACK), F32),
                pltpu.VMEM((2, 3 * SAMPLES, rays), F32),
                pltpu.VMEM((2, SAMPLES, rays), F32),
                pltpu.VMEM((2, rays), jnp.int32),
                pltpu.VMEM((3, rays), F32),
                pltpu.VMEM(w_in.shape, BF16),
                pltpu.VMEM(w_hidden.shape, BF16),
                pltpu.VMEM(w_head.shape, BF16),
                pltpu.SemaphoreType.DMA((6,)),
                pltpu.SemaphoreType.DMA((2, HELD)),
                pltpu.SemaphoreType.DMA((2, HELD)),
                pltpu.SemaphoreType.DMA((7,)),
            ],
            compiler_params=pltpu.CompilerParams(
                collective_id=0, has_side_effects=True, vmem_limit_bytes=56 * 1024 * 1024
            ),
        )(
            jnp.transpose(positions, (1, 2, 0)),
            jnp.transpose(spacing, (1, 2, 0)),
            volume_ids.T,
            target,
            w_in,
            w_hidden,
            w_head,
        )
        color, grad_in, grad_hidden, grad_head = pl.pallas_call(
            hand_over, out_shape=shapes, in_specs=[vmem] * 4, out_specs=[vmem] * 4
        )(*outs)
        return color, jnp.swapaxes(grad_in, 1, 2), grad_hidden, grad_head

    return jax.shard_map(
        local,
        mesh=mesh,
        in_specs=(
            P(("rep", "vol"), None, None),
            P(("rep", "vol"), None, None),
            P(("rep", "vol"), None),
            P(None, ("rep", "vol")),
            P("vol", None, None),
            P("vol", None, None),
            P("vol", None, None),
        ),
        out_specs=(
            P(None, ("rep", "vol")),
            P("vol", None, "rep"),
            P("vol", "rep", None),
            P("vol", None, "rep"),
        ),
        check_vma=False,
    )
```

```python
import functools
import math

import jax
import jax.numpy as jnp
from jax import lax
from jax.experimental import pallas as pl
from jax.experimental.pallas import tpu as pltpu
from jax.sharding import PartitionSpec as P

FREQS = 10
ENC = 64
WIDTH = 256
SAMPLES = 8
CAP = 8
HELD = 4
VALS = 4 * SAMPLES
PACK = 384
HALF = FREQS // 2
MESH = pl.DeviceIdType.MESH
BF16 = jnp.bfloat16
F32 = jnp.float32


def dot(left, right):
    return jnp.dot(left, right, preferred_element_type=F32)


def dot_nt(left, right):
    return lax.dot_general(left, right, (((1,), (1,)), ((), ())), preferred_element_type=F32)


def split3(x, axis):
    high = x.astype(BF16)
    rest = x - high.astype(F32)
    mid = rest.astype(BF16)
    low = (rest - mid.astype(F32)).astype(BF16)
    return jnp.concatenate([high, mid, low], axis=axis)


def sine_cosine(turns):
    x = turns * (math.pi / 2)
    y = x * x
    sin = jnp.full_like(y, 1.0 / math.factorial(13))
    for k in (11, 9, 7, 5, 3, 1):
        sin = (1.0 / math.factorial(k)) - y * sin
    sin = sin * x
    cos = jnp.full_like(y, 1.0 / math.factorial(12))
    for k in (10, 8, 6, 4, 2, 0):
        cos = (1.0 / math.factorial(k)) - y * cos
    return 2.0 * sin * cos, 1.0 - 2.0 * sin * sin


def sigmoid(x):
    return 1.0 / (1.0 + jnp.exp(-x))


def softplus(x):
    e = jnp.exp(-jnp.abs(x))
    small = e * (1.0 - e * (0.5 - e * (1.0 / 3.0)))
    return jnp.maximum(x, 0.0) + jnp.where(e < 1e-2, small, jnp.log(1.0 + e))


def one_hot(rows, row):
    spots = lax.broadcasted_iota(jnp.int32, (rows, row.shape[1]), 0)
    return jnp.where(spots == row, 1.0, 0.0)


def kernel(
    n_rep, n_vol, rays,
    pos_h, gap_h, ids_h, target_h, w_in_h, w_hidden_h, w_head_h,
    out_color, out_in, out_hidden, out_head,
    send_a, recv_a, send_b, recv_b, send_c, recv_c,
    table, feats, enc, act_one, act_two, slope_one, slope_two,
    mine_s, raw_s, gap_s, cot_f, cot_two_s, cot_one_s, turn, table_t,
    w_in_t, w_hidden_t, w_head_p, w_head_w,
    part, pair_in, block_out, block_in, own_block,
    pos, gap, ids, target, w_in, w_hidden, w_head,
    sem, pair_sem, block_sem, load_sem,
):
    me_r, me_v = lax.axis_index("rep"), lax.axis_index("vol")
    n_y = n_rep // 2
    me_y, me_c = me_r // 2, lax.rem(me_r, 2)
    lanes = n_vol * CAP
    segs = 2 * rays
    volumes = n_vol * HELD
    rows = WIDTH // n_rep

    n_x = min(4, n_vol)
    n_z = n_vol // n_x

    def far_first(n):
        return sorted(range(n), key=lambda step: -min(step, n - step))

    zs = [lax.rem(me_v // n_x + step, n_z) * n_x for step in far_first(n_z)]
    xs = [lax.rem(lax.rem(me_v, n_x) + step, n_x) for step in far_first(n_x)]
    vol_peers = [z + x for z in zs for x in xs][:-1]
    y_peers = [lax.rem(me_y + step, n_y) for step in far_first(n_y)][:-1]
    sibling = me_y * 2 + 1 - me_c
    blocks, block = feats.shape[0], feats.shape[2]

    loads = [
        pltpu.make_async_copy(source, place, load_sem.at[number])
        for number, (source, place) in enumerate(
            (
                (ids_h, ids), (pos_h, pos), (gap_h, gap), (w_in_h, w_in),
                (w_hidden_h, w_hidden), (w_head_h, w_head), (target_h, target),
            )
        )
    ]
    barrier = pltpu.get_barrier_semaphore()

    for peer in vol_peers:
        pl.semaphore_signal(barrier, inc=1, device_id=(me_r, peer), device_id_type=MESH)
    for peer in y_peers:
        pl.semaphore_signal(barrier, inc=1, device_id=(peer * 2 + me_c, me_v), device_id_type=MESH)
    pl.semaphore_signal(barrier, inc=1, device_id=(sibling, me_v), device_id_type=MESH)

    for load in loads:
        load.start()
    loads[0].wait()

    id_row = jnp.concatenate([ids[0:1, :], ids[1:2, :]], axis=1)
    hot = one_hot(volumes, id_row)
    before = jnp.where(
        lax.broadcasted_iota(jnp.int32, (rays, rays), 0)
        < lax.broadcasted_iota(jnp.int32, (rays, rays), 1),
        1.0,
        0.0,
    ).astype(BF16)
    hot_0, hot_1 = hot[:, :rays], hot[:, rays:]
    earlier_0 = dot(hot_0.astype(BF16), before)
    earlier_1 = dot(hot_1.astype(BF16), before) + jnp.sum(hot_0, axis=1, keepdims=True)
    rank = jnp.concatenate(
        [
            jnp.sum(earlier_0 * hot_0, axis=0, keepdims=True),
            jnp.sum(earlier_1 * hot_1, axis=0, keepdims=True),
        ],
        axis=1,
    ).astype(jnp.int32)
    owner = lax.shift_right_logical(id_row, 2)
    held = lax.bitwise_and(id_row, 3)
    place_hot = one_hot(lanes, owner * CAP + rank).astype(BF16)
    loads[1].wait()
    loads[2].wait()
    vals = jnp.concatenate(
        [
            jnp.concatenate([pos[0], gap[0]], axis=0),
            jnp.concatenate([pos[1], gap[1]], axis=0),
        ],
        axis=1,
    )
    spread = jnp.concatenate([jnp.where(held == v, vals, 0.0) for v in range(HELD)], axis=0)
    moved = dot_nt(place_hot, split3(spread, 0))
    moved = (moved[:, 0:128] + moved[:, 128:256]) + moved[:, 256:384]
    send_a[...] = moved.reshape(n_vol, CAP, 128)
    recv_a[me_v] = send_a[me_v]
    pl.semaphore_wait(barrier, n_vol - 1 + n_y)

    def exchange(source, landing, number):
        for peer in vol_peers:
            pltpu.make_async_remote_copy(
                src_ref=source.at[peer],
                dst_ref=landing.at[me_v],
                send_sem=sem.at[2 * number],
                recv_sem=sem.at[2 * number + 1],
                device_id=(me_r, peer),
                device_id_type=MESH,
            ).start()

    def await_all(buffer, which):
        span = buffer.at[pl.ds(0, n_vol - 1)]
        pltpu.make_async_copy(span, span, sem.at[which]).wait()

    exchange(send_a, recv_a, 0)

    cot_f[...] = jnp.zeros_like(cot_f)
    turn[...] = jnp.zeros_like(turn)
    w_head_p[...] = jnp.zeros_like(w_head_p)

    for load in loads[3:]:
        load.wait()

    def turn_weights(v, carry):
        w_in_t[v] = w_in[v].astype(F32).T.astype(BF16)
        w_hidden_t[v] = w_hidden[v].astype(F32).T.astype(BF16)
        head = jnp.concatenate([w_head[v].astype(F32), jnp.zeros((124, WIDTH), F32)], axis=0)
        w_head_p[v] = head[0:16].astype(BF16)
        head_t = head.T
        for c in range(4):
            w_head_w[v, c] = jnp.broadcast_to(head_t[:, c : c + 1], (WIDTH, block))
        return carry

    lax.fori_loop(0, HELD, turn_weights, 0)

    await_all(recv_a, 1)
    table[...] = recv_a[...].reshape(lanes, 128).T

    def put(at, values):
        for b in range(blocks):
            feats[b, at : at + values.shape[0], :] = values[:, b * block : (b + 1) * block]

    def forward(v, carry):
        base = pl.multiple_of(v * VALS, VALS)
        points = table[pl.ds(base, 24), :]
        gaps = table[pl.ds(base + 24, 8), :]
        wide = points * (2.0**HALF)
        wide = wide - 2.0 * jnp.floor(wide * 0.5 + 0.5)
        sin_lo, cos_lo = sine_cosine(points)
        sin_hi, cos_hi = sine_cosine(wide)
        for f in range(HALF):
            for offset, sin, cos in ((f, sin_lo, cos_lo), (HALF + f, sin_hi, cos_hi)):
                for c in range(3):
                    at = c * FREQS + offset
                    put(at * 8, sin[c * 8 : c * 8 + 8])
                    put((30 + at) * 8, cos[c * 8 : c * 8 + 8])
            sin_lo, cos_lo = 2.0 * sin_lo * cos_lo, 1.0 - 2.0 * sin_lo * sin_lo
            sin_hi, cos_hi = 2.0 * sin_hi * cos_hi, 1.0 - 2.0 * sin_hi * sin_hi
        put(480, points)
        put(504, jnp.ones((8, lanes), F32))
        for i in range(SAMPLES):
            span = slice(i * lanes, (i + 1) * lanes)
            features = jnp.concatenate(
                [feats[b, pl.ds(i, ENC, stride=8), :] for b in range(blocks)], axis=1
            ).astype(BF16)
            enc[v, :, span] = features
            half = 0.5 * dot(w_in_t[v], features)
            act = (half + half * jnp.tanh(half)).astype(BF16)
            act_one[v, :, span] = act
            half = 0.5 * dot(w_hidden_t[v], act)
            act = (half + half * jnp.tanh(half)).astype(BF16)
            act_two[v, :, span] = act
            gap_s[i, pl.ds(v, 1), :] = gaps[i : i + 1]
        for i in range(SAMPLES):
            raw = dot(w_head_p[v], act_two[v, :, i * lanes : (i + 1) * lanes])
            for c in range(4):
                raw_s[c, i, pl.ds(v, 1), :] = raw[c : c + 1]
        return carry

    lax.fori_loop(0, HELD, forward, 0)

    shade = [[sigmoid(raw_s[c, i]) for i in range(SAMPLES)] for c in range(3)]
    dense_slope, spans, share, clear = [], [], [], []
    depth = jnp.zeros((HELD, lanes), F32)
    through = jnp.ones((HELD, lanes), F32)
    color = [jnp.zeros((HELD, lanes), F32) for _ in range(3)]
    for i in range(SAMPLES):
        raw = raw_s[3, i]
        spacing = gap_s[i]
        tau = softplus(raw) * spacing
        depth = depth + tau
        share.append(through * (1.0 - jnp.exp(-tau)))
        through = jnp.exp(-depth)
        clear.append(through)
        dense_slope.append(sigmoid(raw))
        spans.append(spacing)
        color = [color[c] + share[i] * shade[c][i] for c in range(3)]

    turn[0:16, :] = jnp.concatenate(color + [through], axis=0)
    flipped = turn[...].T
    table_t[...] = flipped
    row_b = jnp.zeros((n_vol, 128), F32)
    for j in range(CAP):
        piece = table_t[pl.ds(j, n_vol, stride=CAP), :]
        row_b = row_b + (piece if j == 0 else pltpu.roll(piece, 16 * j, 1))
    send_b[...] = row_b.reshape(n_vol, 1, 128)
    recv_b[me_v] = send_b[me_v]
    exchange(send_b, recv_b, 1)

    def slopes(v, carry):
        for i in range(SAMPLES):
            span = slice(i * lanes, (i + 1) * lanes)
            for w_t, before_s, after_s, slope_s in (
                (w_in_t, enc, act_one, slope_one),
                (w_hidden_t, act_one, act_two, slope_two),
            ):
                pre = dot(w_t[v], before_s[v, :, span])
                gate = 0.5 + 0.5 * jnp.tanh(0.5 * pre)
                slope_s[v, :, span] = gate + pre * gate * (1.0 - gate)
        return carry

    owner_hot = one_hot(n_vol, owner).astype(BF16)
    spot = lax.broadcasted_iota(jnp.int32, (128, segs), 0)
    mine = jnp.where(lax.bitwise_and(spot, 0x73) == rank * 16 + held, 1.0, 0.0)
    mine_s[...] = mine
    lax.fori_loop(0, HELD // 2, slopes, 0)
    await_all(recv_b, 3)

    mine = mine_s[...]
    arrived = recv_b[...].reshape(n_vol, 128)
    arrived = jnp.concatenate([arrived, jnp.zeros((128 - n_vol, 128), F32)], axis=0)
    arrived_t = arrived.T[:, 0:n_vol]
    found = dot(split3(arrived_t, 1), jnp.concatenate([owner_hot] * 3, axis=0))
    found = found * mine
    total = found[0:16]
    for j in range(1, CAP):
        total = total + found[16 * j : 16 * j + 16]
    per_seg = [jnp.sum(total[4 * c : 4 * c + 4], axis=0, keepdims=True) for c in range(4)]
    carried = per_seg[3][:, :rays]
    behind = jnp.zeros((1, rays), F32)
    cots = []
    for c in range(3):
        near, far = per_seg[c][:, :rays], per_seg[c][:, rays:]
        value = near + carried * far
        out_color[c : c + 1, :] = value
        slope = (value - target[c : c + 1, :]) * (1.0 / n_rep)
        behind = behind + slope * far
        cots.append(jnp.concatenate([slope, carried * slope], axis=1))
    cots.append(jnp.concatenate([behind, jnp.zeros((1, rays), F32)], axis=1))
    cots = jnp.concatenate([jnp.broadcast_to(x, (4, segs)) for x in cots], axis=0)
    cots = jnp.concatenate([cots] * CAP, axis=0) * mine
    row_c = dot_nt(owner_hot, split3(cots, 0))
    row_c = (row_c[:, 0:128] + row_c[:, 128:256]) + row_c[:, 256:384]
    send_c[...] = row_c.reshape(n_vol, 1, 128)
    recv_c[me_v] = send_c[me_v]
    exchange(send_c, recv_c, 2)

    lax.fori_loop(HELD // 2, HELD, slopes, 0)
    await_all(recv_c, 5)

    row_c = recv_c[...].reshape(n_vol, 128)
    for j in range(CAP):
        piece = row_c if j == 0 else pltpu.roll(row_c, 128 - 16 * j, 1)
        table_t[pl.ds(j, n_vol, stride=CAP), :] = piece
    cots = table_t[...].T[0:16]
    cot_color = [cots[4 * c : 4 * c + 4] for c in range(3)]
    later = through * cots[12:16]
    for i in reversed(range(SAMPLES)):
        pull = sum(cot_color[c] * shade[c][i] for c in range(3))
        cot_raw = [
            cot_color[c] * share[i] * (shade[c][i] * (1.0 - shade[c][i])) for c in range(3)
        ]
        cot_raw.append((clear[i] * pull - later) * spans[i] * dense_slope[i])
        later = later + share[i] * pull
        for c in range(4):
            for v in range(HELD):
                cot_f[v, c : c + 1, i * lanes : (i + 1) * lanes] = cot_raw[c][v : v + 1]

    def pair_copy(v):
        return pltpu.make_async_remote_copy(
            src_ref=part.at[v, 1 - me_c],
            dst_ref=pair_in.at[v],
            send_sem=pair_sem.at[0, v],
            recv_sem=pair_sem.at[1, v],
            device_id=(sibling, me_v),
            device_id_type=MESH,
        )

    def pass_on(v):
        pair_copy(v).wait()
        both = part[v, me_c] + pair_in[v]
        block_out[v] = both.astype(BF16)
        own_block[...] = both
        pair_in[v, 0] = own_block[me_y]
        block_in[v, me_y] = jnp.zeros((rows, PACK), BF16)

        for y in y_peers:
            pltpu.make_async_remote_copy(
                src_ref=block_out.at[v, y],
                dst_ref=block_in.at[v, me_y],
                send_sem=block_sem.at[0, v],
                recv_sem=block_sem.at[1, v],
                device_id=(y * 2 + me_c, me_v),
                device_id_type=MESH,
            ).start()

    def backward(v, carry):
        for i in range(SAMPLES):
            span = slice(i * lanes, (i + 1) * lanes)
            cot_raw = cot_f[v, 0:4, span].astype(BF16).astype(F32)
            cot = sum(
                cot_raw[c : c + 1] * jnp.concatenate([w_head_w[v, c]] * blocks, axis=1)
                for c in range(4)
            )
            cot = cot * slope_two[v, :, span]
            cot = cot.astype(BF16)
            cot_two_s[:, span] = cot
            cot = dot(w_hidden[v], cot) * slope_one[v, :, span]
            cot_one_s[:, span] = cot.astype(BF16)
        d_mid = dot_nt(act_one[v], cot_two_s[...])
        d_first = dot_nt(cot_one_s[...], enc[v])
        d_last = dot_nt(cot_f[v].astype(BF16), act_two[v])
        d_last = jnp.concatenate([d_last, jnp.zeros((112, WIDTH), F32)], axis=0).T[:, 0:64]
        side = jnp.concatenate([d_first, d_last], axis=1)
        for r in range(n_rep):
            part[v, r % 2, r // 2, :, 0:WIDTH] = d_mid[r * rows : (r + 1) * rows]
            part[v, r % 2, r // 2, :, WIDTH:PACK] = side[r * rows : (r + 1) * rows]
        pair_copy(v).start()

        @pl.when(v > 0)
        def _():
            pass_on(v - 1)

        return carry

    lax.fori_loop(0, HELD, backward, 0)
    pass_on(HELD - 1)

    heads = []
    for v in range(HELD):
        span = block_in.at[v, pl.ds(0, n_y - 1)]
        pltpu.make_async_copy(span, span, block_sem.at[1, v]).wait()
        whole = pair_in[v, 0]
        for y in range(n_y):
            whole = whole + block_in[v, y].astype(F32)
        out_hidden[v] = whole[:, 0:WIDTH]
        out_in[v] = whole[:, WIDTH : WIDTH + ENC]
        heads.append(whole[:, WIDTH:PACK])
    heads.append(jnp.zeros((max(128 - HELD * rows, 0), 128), F32))
    heads = jnp.concatenate(heads, axis=0).T
    for v in range(HELD):
        out_head[v] = heads[ENC : ENC + 4, v * rows : (v + 1) * rows]

    for number, buffer in ((0, send_a), (1, send_b), (2, send_c)):
        await_all(buffer, 2 * number)
    for v in range(HELD):
        span = block_out.at[v, pl.ds(0, n_y - 1)]
        pltpu.make_async_copy(span, span, block_sem.at[0, v]).wait()


def hand_over(*refs):
    for source, result in zip(refs[:4], refs[4:]):
        result[...] = source[...]


def solution(mesh):
    n_rep, n_vol = mesh.shape["rep"], mesh.shape["vol"]

    def local(positions, spacing, volume_ids, target, w_in, w_hidden, w_head):
        rays = volume_ids.shape[0]
        lanes = n_vol * CAP
        wide = SAMPLES * lanes
        rows = WIDTH // n_rep
        n_y = n_rep // 2
        vmem = pl.BlockSpec(memory_space=pltpu.VMEM)
        shapes = (
            jax.ShapeDtypeStruct((3, rays), F32),
            jax.ShapeDtypeStruct((HELD, rows, ENC), F32),
            jax.ShapeDtypeStruct((HELD, rows, WIDTH), F32),
            jax.ShapeDtypeStruct((HELD, 4, rows), F32),
        )
        outs = pl.pallas_call(
            functools.partial(kernel, n_rep, n_vol, rays),
            out_shape=shapes,
            in_specs=[pl.BlockSpec(memory_space=pl.ANY)] * 7,
            out_specs=[vmem] * 4,
            scratch_shapes=[
                pltpu.VMEM((n_vol, CAP, 128), F32),
                pltpu.VMEM((n_vol, CAP, 128), F32),
                pltpu.VMEM((n_vol, 1, 128), F32),
                pltpu.VMEM((n_vol, 1, 128), F32),
                pltpu.VMEM((n_vol, 1, 128), F32),
                pltpu.VMEM((n_vol, 1, 128), F32),
                pltpu.VMEM((128, lanes), F32),
                pltpu.VMEM((pl.cdiv(lanes, 128), ENC * 8, min(lanes, 128)), F32),
                pltpu.VMEM((HELD, ENC, wide), BF16),
                pltpu.VMEM((HELD, WIDTH, wide), BF16),
                pltpu.VMEM((HELD, WIDTH, wide), BF16),
                pltpu.VMEM((HELD, WIDTH, wide), F32),
                pltpu.VMEM((HELD, WIDTH, wide), F32),
                pltpu.VMEM((128, 2 * rays), F32),
                pltpu.VMEM((4, SAMPLES, HELD, lanes), F32),
                pltpu.VMEM((SAMPLES, HELD, lanes), F32),
                pltpu.VMEM((HELD, 16, wide), F32),
                pltpu.VMEM((WIDTH, wide), BF16),
                pltpu.VMEM((WIDTH, wide), BF16),
                pltpu.VMEM((128, lanes), F32),
                pltpu.VMEM((lanes, 128), F32),
                pltpu.VMEM((HELD, WIDTH, ENC), BF16),
                pltpu.VMEM((HELD, WIDTH, WIDTH), BF16),
                pltpu.VMEM((HELD, 16, WIDTH), BF16),
                pltpu.VMEM((HELD, 4, WIDTH, min(lanes, 128)), F32),
                pltpu.VMEM((HELD, 2, n_y, rows, PACK), F32),
                pltpu.VMEM((HELD, n_y, rows, PACK), F32),
                pltpu.VMEM((HELD, n_y, rows, PACK), BF16),
                pltpu.VMEM((HELD, n_y, rows, PACK), BF16),
                pltpu.VMEM((n_y, rows, PACK), F32),
                pltpu.VMEM((2, 3 * SAMPLES, rays), F32),
                pltpu.VMEM((2, SAMPLES, rays), F32),
                pltpu.VMEM((2, rays), jnp.int32),
                pltpu.VMEM((3, rays), F32),
                pltpu.VMEM(w_in.shape, BF16),
                pltpu.VMEM(w_hidden.shape, BF16),
                pltpu.VMEM(w_head.shape, BF16),
                pltpu.SemaphoreType.DMA((6,)),
                pltpu.SemaphoreType.DMA((2, HELD)),
                pltpu.SemaphoreType.DMA((2, HELD)),
                pltpu.SemaphoreType.DMA((7,)),
            ],
            compiler_params=pltpu.CompilerParams(
                collective_id=0, has_side_effects=True, vmem_limit_bytes=56 * 1024 * 1024
            ),
        )(
            jnp.transpose(positions, (1, 2, 0)),
            jnp.transpose(spacing, (1, 2, 0)),
            volume_ids.T,
            target,
            w_in,
            w_hidden,
            w_head,
        )
        color, grad_in, grad_hidden, grad_head = pl.pallas_call(
            hand_over, out_shape=shapes, in_specs=[vmem] * 4, out_specs=[vmem] * 4
        )(*outs)
        return color, jnp.swapaxes(grad_in, 1, 2), grad_hidden, grad_head

    return jax.shard_map(
        local,
        mesh=mesh,
        in_specs=(
            P(("rep", "vol"), None, None),
            P(("rep", "vol"), None, None),
            P(("rep", "vol"), None),
            P(None, ("rep", "vol")),
            P("vol", None, None),
            P("vol", None, None),
            P("vol", None, None),
        ),
        out_specs=(
            P(None, ("rep", "vol")),
            P("vol", None, "rep"),
            P("vol", "rep", None),
            P("vol", None, "rep"),
        ),
        check_vma=False,
    )
```

```python
import functools
import math

import jax
import jax.numpy as jnp
from jax import lax
from jax.experimental import pallas as pl
from jax.experimental.pallas import tpu as pltpu
from jax.sharding import PartitionSpec as P

FREQS = 10
ENC = 64
WIDTH = 256
SAMPLES = 8
CAP = 8
HELD = 4
VALS = 4 * SAMPLES
PACK = 384
HALF = FREQS // 2
MESH = pl.DeviceIdType.MESH
BF16 = jnp.bfloat16
F32 = jnp.float32


def dot(left, right):
    return jnp.dot(left, right, preferred_element_type=F32)


def dot_nt(left, right):
    return lax.dot_general(left, right, (((1,), (1,)), ((), ())), preferred_element_type=F32)


def split3(x, axis):
    high = x.astype(BF16)
    rest = x - high.astype(F32)
    mid = rest.astype(BF16)
    low = (rest - mid.astype(F32)).astype(BF16)
    return jnp.concatenate([high, mid, low], axis=axis)


def sine_cosine(turns):
    x = turns * (math.pi / 2)
    y = x * x
    sin = jnp.full_like(y, 1.0 / math.factorial(13))
    for k in (11, 9, 7, 5, 3, 1):
        sin = (1.0 / math.factorial(k)) - y * sin
    sin = sin * x
    cos = jnp.full_like(y, 1.0 / math.factorial(12))
    for k in (10, 8, 6, 4, 2, 0):
        cos = (1.0 / math.factorial(k)) - y * cos
    return 2.0 * sin * cos, 1.0 - 2.0 * sin * sin


def sigmoid(x):
    return 1.0 / (1.0 + jnp.exp(-x))


def softplus(x):
    e = jnp.exp(-jnp.abs(x))
    small = e * (1.0 - e * (0.5 - e * (1.0 / 3.0)))
    return jnp.maximum(x, 0.0) + jnp.where(e < 1e-2, small, jnp.log(1.0 + e))


def one_hot(rows, row):
    spots = lax.broadcasted_iota(jnp.int32, (rows, row.shape[1]), 0)
    return jnp.where(spots == row, 1.0, 0.0)


def kernel(
    n_rep, n_vol, rays,
    pos_h, gap_h, ids_h, target_h, w_in_h, w_hidden_h, w_head_h,
    out_color, out_in, out_hidden, out_head,
    send_a, recv_a, send_b, recv_b, send_c, recv_c,
    table, feats, enc, act_one, act_two, slope_one, slope_two,
    mine_s, raw_s, gap_s, cot_f, cot_two_s, cot_one_s, turn, table_t,
    w_in_t, w_hidden_t, w_head_p, w_head_w,
    part, pair_in, block_out, block_in, own_block,
    pos, gap, ids, target, w_in, w_hidden, w_head,
    sem, pair_sem, block_sem, load_sem,
):
    me_r, me_v = lax.axis_index("rep"), lax.axis_index("vol")
    n_y = n_rep // 2
    me_y, me_c = me_r // 2, lax.rem(me_r, 2)
    lanes = n_vol * CAP
    segs = 2 * rays
    volumes = n_vol * HELD
    rows = WIDTH // n_rep

    n_x = min(4, n_vol)
    n_z = n_vol // n_x

    def far_first(n):
        return sorted(range(n), key=lambda step: -min(step, n - step))

    zs = [lax.rem(me_v // n_x + step, n_z) * n_x for step in far_first(n_z)]
    xs = [lax.rem(lax.rem(me_v, n_x) + step, n_x) for step in far_first(n_x)]
    vol_peers = [z + x for z in zs for x in xs][:-1]
    y_peers = [lax.rem(me_y + step, n_y) for step in far_first(n_y)][:-1]
    sibling = me_y * 2 + 1 - me_c
    blocks, block = feats.shape[0], feats.shape[2]

    loads = [
        pltpu.make_async_copy(source, place, load_sem.at[number])
        for number, (source, place) in enumerate(
            (
                (ids_h, ids), (pos_h, pos), (gap_h, gap), (w_in_h, w_in),
                (w_hidden_h, w_hidden), (w_head_h, w_head), (target_h, target),
            )
        )
    ]
    barrier = pltpu.get_barrier_semaphore()

    for peer in vol_peers:
        pl.semaphore_signal(barrier, inc=1, device_id=(me_r, peer), device_id_type=MESH)
    for peer in y_peers:
        pl.semaphore_signal(barrier, inc=1, device_id=(peer * 2 + me_c, me_v), device_id_type=MESH)
    pl.semaphore_signal(barrier, inc=1, device_id=(sibling, me_v), device_id_type=MESH)

    for load in loads:
        load.start()
    loads[0].wait()

    id_row = jnp.concatenate([ids[0:1, :], ids[1:2, :]], axis=1)
    hot = one_hot(volumes, id_row)
    before = jnp.where(
        lax.broadcasted_iota(jnp.int32, (rays, rays), 0)
        < lax.broadcasted_iota(jnp.int32, (rays, rays), 1),
        1.0,
        0.0,
    ).astype(BF16)
    hot_0, hot_1 = hot[:, :rays], hot[:, rays:]
    earlier_0 = dot(hot_0.astype(BF16), before)
    earlier_1 = dot(hot_1.astype(BF16), before) + jnp.sum(hot_0, axis=1, keepdims=True)
    rank = jnp.concatenate(
        [
            jnp.sum(earlier_0 * hot_0, axis=0, keepdims=True),
            jnp.sum(earlier_1 * hot_1, axis=0, keepdims=True),
        ],
        axis=1,
    ).astype(jnp.int32)
    owner = lax.shift_right_logical(id_row, 2)
    held = lax.bitwise_and(id_row, 3)
    place_hot = one_hot(lanes, owner * CAP + rank).astype(BF16)
    loads[1].wait()
    loads[2].wait()
    vals = jnp.concatenate(
        [
            jnp.concatenate([pos[0], gap[0]], axis=0),
            jnp.concatenate([pos[1], gap[1]], axis=0),
        ],
        axis=1,
    )
    spread = jnp.concatenate([jnp.where(held == v, vals, 0.0) for v in range(HELD)], axis=0)
    moved = dot_nt(place_hot, split3(spread, 0))
    moved = (moved[:, 0:128] + moved[:, 128:256]) + moved[:, 256:384]
    send_a[...] = moved.reshape(n_vol, CAP, 128)
    recv_a[me_v] = send_a[me_v]
    pl.semaphore_wait(barrier, n_vol - 1 + n_y)

    def exchange(source, landing, number):
        for peer in vol_peers:
            pltpu.make_async_remote_copy(
                src_ref=source.at[peer],
                dst_ref=landing.at[me_v],
                send_sem=sem.at[2 * number],
                recv_sem=sem.at[2 * number + 1],
                device_id=(me_r, peer),
                device_id_type=MESH,
            ).start()

    def await_all(buffer, which):
        span = buffer.at[pl.ds(0, n_vol - 1)]
        pltpu.make_async_copy(span, span, sem.at[which]).wait()

    exchange(send_a, recv_a, 0)

    cot_f[...] = jnp.zeros_like(cot_f)
    turn[...] = jnp.zeros_like(turn)
    w_head_p[...] = jnp.zeros_like(w_head_p)

    for load in loads[3:]:
        load.wait()

    def turn_weights(v, carry):
        w_in_t[v] = (0.5 * w_in[v].astype(F32).T).astype(BF16)
        w_hidden_t[v] = (0.5 * w_hidden[v].astype(F32).T).astype(BF16)
        head = jnp.concatenate([w_head[v].astype(F32), jnp.zeros((124, WIDTH), F32)], axis=0)
        w_head_p[v] = head[0:16].astype(BF16)
        head_t = head.T
        for c in range(4):
            w_head_w[v, c] = jnp.broadcast_to(head_t[:, c : c + 1], (WIDTH, block))
        return carry

    lax.fori_loop(0, HELD, turn_weights, 0)

    await_all(recv_a, 1)
    table[...] = recv_a[...].reshape(lanes, 128).T

    def put(at, values):
        for b in range(blocks):
            feats[b, at : at + values.shape[0], :] = values[:, b * block : (b + 1) * block]

    def forward(v, carry):
        base = pl.multiple_of(v * VALS, VALS)
        points = table[pl.ds(base, 24), :]
        gaps = table[pl.ds(base + 24, 8), :]
        wide = points * (2.0**HALF)
        wide = wide - 2.0 * jnp.floor(wide * 0.5 + 0.5)
        sin_lo, cos_lo = sine_cosine(points)
        sin_hi, cos_hi = sine_cosine(wide)
        for f in range(HALF):
            for offset, sin, cos in ((f, sin_lo, cos_lo), (HALF + f, sin_hi, cos_hi)):
                for c in range(3):
                    at = c * FREQS + offset
                    put(at * 8, sin[c * 8 : c * 8 + 8])
                    put((30 + at) * 8, cos[c * 8 : c * 8 + 8])
            sin_lo, cos_lo = 2.0 * sin_lo * cos_lo, 1.0 - 2.0 * sin_lo * sin_lo
            sin_hi, cos_hi = 2.0 * sin_hi * cos_hi, 1.0 - 2.0 * sin_hi * sin_hi
        put(480, points)
        put(504, jnp.ones((8, lanes), F32))
        for i in range(SAMPLES):
            span = slice(i * lanes, (i + 1) * lanes)
            features = jnp.concatenate(
                [feats[b, pl.ds(i, ENC, stride=8), :] for b in range(blocks)], axis=1
            ).astype(BF16)
            enc[v, :, span] = features
            half = dot(w_in_t[v], features)
            act = (half + half * jnp.tanh(half)).astype(BF16)
            act_one[v, :, span] = act
            half = dot(w_hidden_t[v], act)
            act = (half + half * jnp.tanh(half)).astype(BF16)
            act_two[v, :, span] = act
            gap_s[i, pl.ds(v, 1), :] = gaps[i : i + 1]
        for i in range(SAMPLES):
            raw = dot(w_head_p[v], act_two[v, :, i * lanes : (i + 1) * lanes])
            for c in range(4):
                raw_s[c, i, pl.ds(v, 1), :] = raw[c : c + 1]
        return carry

    lax.fori_loop(0, HELD, forward, 0)

    shade = [[sigmoid(raw_s[c, i]) for i in range(SAMPLES)] for c in range(3)]
    spans, share, clear = [], [], []
    depth = jnp.zeros((HELD, lanes), F32)
    through = jnp.ones((HELD, lanes), F32)
    color = [jnp.zeros((HELD, lanes), F32) for _ in range(3)]
    for i in range(SAMPLES):
        raw = raw_s[3, i]
        spacing = gap_s[i]
        tau = softplus(raw) * spacing
        depth = depth + tau
        share.append(through * (1.0 - jnp.exp(-tau)))
        through = jnp.exp(-depth)
        clear.append(through)
        spans.append(spacing)
        color = [color[c] + share[i] * shade[c][i] for c in range(3)]

    turn[0:16, :] = jnp.concatenate(color + [through], axis=0)
    flipped = turn[...].T
    table_t[...] = flipped
    row_b = jnp.zeros((n_vol, 128), F32)
    for j in range(CAP):
        piece = table_t[pl.ds(j, n_vol, stride=CAP), :]
        row_b = row_b + (piece if j == 0 else pltpu.roll(piece, 16 * j, 1))
    send_b[...] = row_b.reshape(n_vol, 1, 128)
    recv_b[me_v] = send_b[me_v]
    exchange(send_b, recv_b, 1)

    dense_slope = [spans[i] * sigmoid(raw_s[3, i]) for i in range(SAMPLES)]
    color_slope = [
        [share[i] * (shade[c][i] * (1.0 - shade[c][i])) for i in range(SAMPLES)] for c in range(3)
    ]

    def slopes(v, carry):
        for i in range(SAMPLES):
            span = slice(i * lanes, (i + 1) * lanes)
            for w_t, before_s, after_s, slope_s in (
                (w_in_t, enc, act_one, slope_one),
                (w_hidden_t, act_one, act_two, slope_two),
            ):
                half = dot(w_t[v], before_s[v, :, span])
                turned = jnp.tanh(half)
                slope_s[v, :, span] = 0.5 * (1.0 + turned + half * (1.0 - turned * turned))
        return carry

    owner_hot = one_hot(n_vol, owner).astype(BF16)
    spot = lax.broadcasted_iota(jnp.int32, (128, segs), 0)
    mine = jnp.where(lax.bitwise_and(spot, 0x73) == rank * 16 + held, 1.0, 0.0)
    mine_s[...] = mine
    lax.fori_loop(0, HELD // 2, slopes, 0)
    await_all(recv_b, 3)

    mine = mine_s[...]
    arrived = recv_b[...].reshape(n_vol, 128)
    arrived = jnp.concatenate([arrived, jnp.zeros((128 - n_vol, 128), F32)], axis=0)
    arrived_t = arrived.T[:, 0:n_vol]
    found = dot(split3(arrived_t, 1), jnp.concatenate([owner_hot] * 3, axis=0))
    found = found * mine
    total = found[0:16]
    for j in range(1, CAP):
        total = total + found[16 * j : 16 * j + 16]
    per_seg = [jnp.sum(total[4 * c : 4 * c + 4], axis=0, keepdims=True) for c in range(4)]
    carried = per_seg[3][:, :rays]
    behind = jnp.zeros((1, rays), F32)
    cots = []
    for c in range(3):
        near, far = per_seg[c][:, :rays], per_seg[c][:, rays:]
        value = near + carried * far
        out_color[c : c + 1, :] = value
        slope = (value - target[c : c + 1, :]) * (1.0 / n_rep)
        behind = behind + slope * far
        cots.append(jnp.concatenate([slope, carried * slope], axis=1))
    cots.append(jnp.concatenate([behind, jnp.zeros((1, rays), F32)], axis=1))
    cots = jnp.concatenate([jnp.broadcast_to(x, (4, segs)) for x in cots], axis=0)
    cots = jnp.concatenate([cots] * CAP, axis=0) * mine
    row_c = dot_nt(owner_hot, split3(cots, 0))
    row_c = (row_c[:, 0:128] + row_c[:, 128:256]) + row_c[:, 256:384]
    send_c[...] = row_c.reshape(n_vol, 1, 128)
    recv_c[me_v] = send_c[me_v]
    exchange(send_c, recv_c, 2)

    lax.fori_loop(HELD // 2, HELD, slopes, 0)
    await_all(recv_c, 5)

    row_c = recv_c[...].reshape(n_vol, 128)
    for j in range(CAP):
        piece = row_c if j == 0 else pltpu.roll(row_c, 128 - 16 * j, 1)
        table_t[pl.ds(j, n_vol, stride=CAP), :] = piece
    cots = table_t[...].T[0:16]
    cot_color = [cots[4 * c : 4 * c + 4] for c in range(3)]
    later = through * cots[12:16]
    for i in reversed(range(SAMPLES)):
        pull = sum(cot_color[c] * shade[c][i] for c in range(3))
        cot_raw = [cot_color[c] * color_slope[c][i] for c in range(3)]
        cot_raw.append((clear[i] * pull - later) * dense_slope[i])
        later = later + share[i] * pull
        for c in range(4):
            for v in range(HELD):
                cot_f[v, c : c + 1, i * lanes : (i + 1) * lanes] = cot_raw[c][v : v + 1]

    def pair_copy(v):
        return pltpu.make_async_remote_copy(
            src_ref=part.at[v, 1 - me_c],
            dst_ref=pair_in.at[v],
            send_sem=pair_sem.at[0, v],
            recv_sem=pair_sem.at[1, v],
            device_id=(sibling, me_v),
            device_id_type=MESH,
        )

    def pass_on(v):
        pair_copy(v).wait()
        both = part[v, me_c] + pair_in[v]
        block_out[v] = both.astype(BF16)
        own_block[...] = both
        pair_in[v, 0] = own_block[me_y]
        block_in[v, me_y] = jnp.zeros((rows, PACK), BF16)

        for y in y_peers:
            pltpu.make_async_remote_copy(
                src_ref=block_out.at[v, y],
                dst_ref=block_in.at[v, me_y],
                send_sem=block_sem.at[0, v],
                recv_sem=block_sem.at[1, v],
                device_id=(y * 2 + me_c, me_v),
                device_id_type=MESH,
            ).start()

    def backward(v, carry):
        for i in range(SAMPLES):
            span = slice(i * lanes, (i + 1) * lanes)
            cot_raw = cot_f[v, 0:4, span].astype(BF16).astype(F32)
            cot = sum(
                cot_raw[c : c + 1] * jnp.concatenate([w_head_w[v, c]] * blocks, axis=1)
                for c in range(4)
            )
            cot = cot * slope_two[v, :, span]
            cot = cot.astype(BF16)
            cot_two_s[:, span] = cot
            cot = dot(w_hidden[v], cot) * slope_one[v, :, span]
            cot_one_s[:, span] = cot.astype(BF16)
        d_mid = dot_nt(act_one[v], cot_two_s[...])
        d_first = dot_nt(cot_one_s[...], enc[v])
        d_last = dot_nt(cot_f[v].astype(BF16), act_two[v])
        d_last = jnp.concatenate([d_last, jnp.zeros((112, WIDTH), F32)], axis=0).T[:, 0:64]
        side = jnp.concatenate([d_first, d_last], axis=1)
        for r in range(n_rep):
            part[v, r % 2, r // 2, :, 0:WIDTH] = d_mid[r * rows : (r + 1) * rows]
            part[v, r % 2, r // 2, :, WIDTH:PACK] = side[r * rows : (r + 1) * rows]
        pair_copy(v).start()

        @pl.when(v > 0)
        def _():
            pass_on(v - 1)

        return carry

    lax.fori_loop(0, HELD, backward, 0)
    pass_on(HELD - 1)

    heads = []
    for v in range(HELD):
        span = block_in.at[v, pl.ds(0, n_y - 1)]
        pltpu.make_async_copy(span, span, block_sem.at[1, v]).wait()
        whole = pair_in[v, 0]
        for y in range(n_y):
            whole = whole + block_in[v, y].astype(F32)
        out_hidden[v] = whole[:, 0:WIDTH]
        out_in[v] = whole[:, WIDTH : WIDTH + ENC]
        heads.append(whole[:, WIDTH:PACK])
    heads.append(jnp.zeros((max(128 - HELD * rows, 0), 128), F32))
    heads = jnp.concatenate(heads, axis=0).T
    for v in range(HELD):
        out_head[v] = heads[ENC : ENC + 4, v * rows : (v + 1) * rows]

    for number, buffer in ((0, send_a), (1, send_b), (2, send_c)):
        await_all(buffer, 2 * number)
    for v in range(HELD):
        span = block_out.at[v, pl.ds(0, n_y - 1)]
        pltpu.make_async_copy(span, span, block_sem.at[0, v]).wait()


def hand_over(*refs):
    for source, result in zip(refs[:4], refs[4:]):
        result[...] = source[...]


def solution(mesh):
    n_rep, n_vol = mesh.shape["rep"], mesh.shape["vol"]

    def local(positions, spacing, volume_ids, target, w_in, w_hidden, w_head):
        rays = volume_ids.shape[0]
        lanes = n_vol * CAP
        wide = SAMPLES * lanes
        rows = WIDTH // n_rep
        n_y = n_rep // 2
        vmem = pl.BlockSpec(memory_space=pltpu.VMEM)
        shapes = (
            jax.ShapeDtypeStruct((3, rays), F32),
            jax.ShapeDtypeStruct((HELD, rows, ENC), F32),
            jax.ShapeDtypeStruct((HELD, rows, WIDTH), F32),
            jax.ShapeDtypeStruct((HELD, 4, rows), F32),
        )
        outs = pl.pallas_call(
            functools.partial(kernel, n_rep, n_vol, rays),
            out_shape=shapes,
            in_specs=[pl.BlockSpec(memory_space=pl.ANY)] * 7,
            out_specs=[vmem] * 4,
            scratch_shapes=[
                pltpu.VMEM((n_vol, CAP, 128), F32),
                pltpu.VMEM((n_vol, CAP, 128), F32),
                pltpu.VMEM((n_vol, 1, 128), F32),
                pltpu.VMEM((n_vol, 1, 128), F32),
                pltpu.VMEM((n_vol, 1, 128), F32),
                pltpu.VMEM((n_vol, 1, 128), F32),
                pltpu.VMEM((128, lanes), F32),
                pltpu.VMEM((pl.cdiv(lanes, 128), ENC * 8, min(lanes, 128)), F32),
                pltpu.VMEM((HELD, ENC, wide), BF16),
                pltpu.VMEM((HELD, WIDTH, wide), BF16),
                pltpu.VMEM((HELD, WIDTH, wide), BF16),
                pltpu.VMEM((HELD, WIDTH, wide), F32),
                pltpu.VMEM((HELD, WIDTH, wide), F32),
                pltpu.VMEM((128, 2 * rays), F32),
                pltpu.VMEM((4, SAMPLES, HELD, lanes), F32),
                pltpu.VMEM((SAMPLES, HELD, lanes), F32),
                pltpu.VMEM((HELD, 16, wide), F32),
                pltpu.VMEM((WIDTH, wide), BF16),
                pltpu.VMEM((WIDTH, wide), BF16),
                pltpu.VMEM((128, lanes), F32),
                pltpu.VMEM((lanes, 128), F32),
                pltpu.VMEM((HELD, WIDTH, ENC), BF16),
                pltpu.VMEM((HELD, WIDTH, WIDTH), BF16),
                pltpu.VMEM((HELD, 16, WIDTH), BF16),
                pltpu.VMEM((HELD, 4, WIDTH, min(lanes, 128)), F32),
                pltpu.VMEM((HELD, 2, n_y, rows, PACK), F32),
                pltpu.VMEM((HELD, n_y, rows, PACK), F32),
                pltpu.VMEM((HELD, n_y, rows, PACK), BF16),
                pltpu.VMEM((HELD, n_y, rows, PACK), BF16),
                pltpu.VMEM((n_y, rows, PACK), F32),
                pltpu.VMEM((2, 3 * SAMPLES, rays), F32),
                pltpu.VMEM((2, SAMPLES, rays), F32),
                pltpu.VMEM((2, rays), jnp.int32),
                pltpu.VMEM((3, rays), F32),
                pltpu.VMEM(w_in.shape, BF16),
                pltpu.VMEM(w_hidden.shape, BF16),
                pltpu.VMEM(w_head.shape, BF16),
                pltpu.SemaphoreType.DMA((6,)),
                pltpu.SemaphoreType.DMA((2, HELD)),
                pltpu.SemaphoreType.DMA((2, HELD)),
                pltpu.SemaphoreType.DMA((7,)),
            ],
            compiler_params=pltpu.CompilerParams(
                collective_id=0, has_side_effects=True, vmem_limit_bytes=56 * 1024 * 1024
            ),
        )(
            jnp.transpose(positions, (1, 2, 0)),
            jnp.transpose(spacing, (1, 2, 0)),
            volume_ids.T,
            target,
            w_in,
            w_hidden,
            w_head,
        )
        color, grad_in, grad_hidden, grad_head = pl.pallas_call(
            hand_over, out_shape=shapes, in_specs=[vmem] * 4, out_specs=[vmem] * 4
        )(*outs)
        return color, jnp.swapaxes(grad_in, 1, 2), grad_hidden, grad_head

    return jax.shard_map(
        local,
        mesh=mesh,
        in_specs=(
            P(("rep", "vol"), None, None),
            P(("rep", "vol"), None, None),
            P(("rep", "vol"), None),
            P(None, ("rep", "vol")),
            P("vol", None, None),
            P("vol", None, None),
            P("vol", None, None),
        ),
        out_specs=(
            P(None, ("rep", "vol")),
            P("vol", None, "rep"),
            P("vol", "rep", None),
            P("vol", None, "rep"),
        ),
        check_vma=False,
    )
```

```python
import functools
import math

import jax
import jax.numpy as jnp
from jax import lax
from jax.experimental import pallas as pl
from jax.experimental.pallas import tpu as pltpu
from jax.sharding import PartitionSpec as P

FREQS = 10
ENC = 64
WIDTH = 256
SAMPLES = 8
CAP = 8
HELD = 4
VALS = 4 * SAMPLES
PACK = 384
HALF = FREQS // 2
MESH = pl.DeviceIdType.MESH
BF16 = jnp.bfloat16
F32 = jnp.float32


def dot(left, right):
    return jnp.dot(left, right, preferred_element_type=F32)


def dot_nt(left, right):
    return lax.dot_general(left, right, (((1,), (1,)), ((), ())), preferred_element_type=F32)


def split3(x, axis):
    high = x.astype(BF16)
    rest = x - high.astype(F32)
    mid = rest.astype(BF16)
    low = (rest - mid.astype(F32)).astype(BF16)
    return jnp.concatenate([high, mid, low], axis=axis)


def sine_cosine(turns):
    x = turns * (math.pi / 2)
    y = x * x
    sin = jnp.full_like(y, 1.0 / math.factorial(13))
    for k in (11, 9, 7, 5, 3, 1):
        sin = (1.0 / math.factorial(k)) - y * sin
    sin = sin * x
    cos = jnp.full_like(y, 1.0 / math.factorial(12))
    for k in (10, 8, 6, 4, 2, 0):
        cos = (1.0 / math.factorial(k)) - y * cos
    return 2.0 * sin * cos, 1.0 - 2.0 * sin * sin


def sigmoid(x):
    return 1.0 / (1.0 + jnp.exp(-x))


def softplus(x):
    e = jnp.exp(-jnp.abs(x))
    small = e * (1.0 - e * (0.5 - e * (1.0 / 3.0)))
    return jnp.maximum(x, 0.0) + jnp.where(e < 1e-2, small, jnp.log(1.0 + e))


def one_hot(rows, row):
    spots = lax.broadcasted_iota(jnp.int32, (rows, row.shape[1]), 0)
    return jnp.where(spots == row, 1.0, 0.0)


def kernel(
    n_rep, n_vol, rays,
    pos_h, gap_h, ids_h, target_h, w_in_h, w_hidden_h, w_head_h,
    out_color, out_in, out_hidden, out_head,
    send_a, recv_a, send_b, recv_b, send_c, recv_c,
    table, feats, enc, act_one, act_two, slope_one, slope_two,
    mine_s, raw_s, gap_s, cot_f, cot_two_s, cot_one_s, turn, table_t,
    w_in_t, w_hidden_t, w_head_p, w_head_w,
    part, pair_in, block_out, block_in, own_block,
    pos, gap, ids, target, w_in, w_hidden, w_head,
    sem, pair_sem, block_sem, load_sem,
):
    me_r, me_v = lax.axis_index("rep"), lax.axis_index("vol")
    n_y = n_rep // 2
    me_y, me_c = me_r // 2, lax.rem(me_r, 2)
    lanes = n_vol * CAP
    segs = 2 * rays
    volumes = n_vol * HELD
    rows = WIDTH // n_rep

    n_x = min(4, n_vol)
    n_z = n_vol // n_x

    def far_first(n):
        return sorted(range(n), key=lambda step: -min(step, n - step))

    zs = [lax.rem(me_v // n_x + step, n_z) * n_x for step in far_first(n_z)]
    xs = [lax.rem(lax.rem(me_v, n_x) + step, n_x) for step in far_first(n_x)]
    vol_peers = [z + x for z in zs for x in xs][:-1]
    y_peers = [lax.rem(me_y + step, n_y) for step in far_first(n_y)][:-1]
    sibling = me_y * 2 + 1 - me_c
    blocks, block = feats.shape[0], feats.shape[2]

    loads = [
        pltpu.make_async_copy(source, place, load_sem.at[number])
        for number, (source, place) in enumerate(
            (
                (ids_h, ids), (pos_h, pos), (gap_h, gap), (w_in_h, w_in),
                (w_hidden_h, w_hidden), (w_head_h, w_head), (target_h, target),
            )
        )
    ]
    barrier = pltpu.get_barrier_semaphore()

    for peer in vol_peers:
        pl.semaphore_signal(barrier, inc=1, device_id=(me_r, peer), device_id_type=MESH)
    for peer in y_peers:
        pl.semaphore_signal(barrier, inc=1, device_id=(peer * 2 + me_c, me_v), device_id_type=MESH)
    pl.semaphore_signal(barrier, inc=1, device_id=(sibling, me_v), device_id_type=MESH)

    for load in loads:
        load.start()
    loads[0].wait()

    id_row = jnp.concatenate([ids[0:1, :], ids[1:2, :]], axis=1)
    hot = one_hot(volumes, id_row)
    before = jnp.where(
        lax.broadcasted_iota(jnp.int32, (rays, rays), 0)
        < lax.broadcasted_iota(jnp.int32, (rays, rays), 1),
        1.0,
        0.0,
    ).astype(BF16)
    hot_0, hot_1 = hot[:, :rays], hot[:, rays:]
    earlier_0 = dot(hot_0.astype(BF16), before)
    earlier_1 = dot(hot_1.astype(BF16), before) + jnp.sum(hot_0, axis=1, keepdims=True)
    rank = jnp.concatenate(
        [
            jnp.sum(earlier_0 * hot_0, axis=0, keepdims=True),
            jnp.sum(earlier_1 * hot_1, axis=0, keepdims=True),
        ],
        axis=1,
    ).astype(jnp.int32)
    owner = lax.shift_right_logical(id_row, 2)
    held = lax.bitwise_and(id_row, 3)
    place_hot = one_hot(lanes, owner * CAP + rank).astype(BF16)
    loads[1].wait()
    loads[2].wait()
    vals = jnp.concatenate(
        [
            jnp.concatenate([pos[0], gap[0]], axis=0),
            jnp.concatenate([pos[1], gap[1]], axis=0),
        ],
        axis=1,
    )
    spread = jnp.concatenate([jnp.where(held == v, vals, 0.0) for v in range(HELD)], axis=0)
    moved = dot_nt(place_hot, split3(spread, 0))
    moved = (moved[:, 0:128] + moved[:, 128:256]) + moved[:, 256:384]
    send_a[...] = moved.reshape(n_vol, CAP, 128)
    recv_a[me_v] = send_a[me_v]
    pl.semaphore_wait(barrier, n_vol - 1 + n_y)

    def exchange(source, landing, number):
        for peer in vol_peers:
            pltpu.make_async_remote_copy(
                src_ref=source.at[peer],
                dst_ref=landing.at[me_v],
                send_sem=sem.at[2 * number],
                recv_sem=sem.at[2 * number + 1],
                device_id=(me_r, peer),
                device_id_type=MESH,
            ).start()

    def await_all(buffer, which):
        span = buffer.at[pl.ds(0, n_vol - 1)]
        pltpu.make_async_copy(span, span, sem.at[which]).wait()

    exchange(send_a, recv_a, 0)

    cot_f[...] = jnp.zeros_like(cot_f)
    turn[...] = jnp.zeros_like(turn)
    w_head_p[...] = jnp.zeros_like(w_head_p)

    for load in loads[3:]:
        load.wait()

    def turn_weights(v, carry):
        w_in_t[v] = (0.5 * w_in[v].astype(F32).T).astype(BF16)
        w_hidden_t[v] = (0.5 * w_hidden[v].astype(F32).T).astype(BF16)
        head = jnp.concatenate([w_head[v].astype(F32), jnp.zeros((124, WIDTH), F32)], axis=0)
        w_head_p[v] = head[0:16].astype(BF16)
        head_t = head.T
        for c in range(4):
            w_head_w[v, c] = jnp.broadcast_to(head_t[:, c : c + 1], (WIDTH, block))
        return carry

    lax.fori_loop(0, HELD, turn_weights, 0)

    await_all(recv_a, 1)
    table[...] = recv_a[...].reshape(lanes, 128).T

    def put(at, values):
        for b in range(blocks):
            feats[b, at : at + values.shape[0], :] = values[:, b * block : (b + 1) * block]

    def forward(v, carry):
        base = pl.multiple_of(v * VALS, VALS)
        points = table[pl.ds(base, 24), :]
        gaps = table[pl.ds(base + 24, 8), :]
        wide = points * (2.0**HALF)
        wide = wide - 2.0 * jnp.floor(wide * 0.5 + 0.5)
        sin_lo, cos_lo = sine_cosine(points)
        sin_hi, cos_hi = sine_cosine(wide)
        for f in range(HALF):
            for offset, sin, cos in ((f, sin_lo, cos_lo), (HALF + f, sin_hi, cos_hi)):
                for c in range(3):
                    at = c * FREQS + offset
                    put(at * 8, sin[c * 8 : c * 8 + 8])
                    put((30 + at) * 8, cos[c * 8 : c * 8 + 8])
            sin_lo, cos_lo = 2.0 * sin_lo * cos_lo, 1.0 - 2.0 * sin_lo * sin_lo
            sin_hi, cos_hi = 2.0 * sin_hi * cos_hi, 1.0 - 2.0 * sin_hi * sin_hi
        put(480, points)
        put(504, jnp.ones((8, lanes), F32))
        for i in range(SAMPLES):
            span = slice(i * lanes, (i + 1) * lanes)
            features = jnp.concatenate(
                [feats[b, pl.ds(i, ENC, stride=8), :] for b in range(blocks)], axis=1
            ).astype(BF16)
            enc[v, :, span] = features
            half = dot(w_in_t[v], features)
            act = (half + half * jnp.tanh(half)).astype(BF16)
            act_one[v, :, span] = act
            half = dot(w_hidden_t[v], act)
            act = (half + half * jnp.tanh(half)).astype(BF16)
            act_two[v, :, span] = act
            gap_s[i, pl.ds(v, 1), :] = gaps[i : i + 1]
        for i in range(SAMPLES):
            raw = dot(w_head_p[v], act_two[v, :, i * lanes : (i + 1) * lanes])
            for c in range(4):
                raw_s[c, i, pl.ds(v, 1), :] = raw[c : c + 1]
        return carry

    lax.fori_loop(0, HELD, forward, 0, unroll=True)

    shade = [[sigmoid(raw_s[c, i]) for i in range(SAMPLES)] for c in range(3)]
    spans, share, clear = [], [], []
    depth = jnp.zeros((HELD, lanes), F32)
    through = jnp.ones((HELD, lanes), F32)
    color = [jnp.zeros((HELD, lanes), F32) for _ in range(3)]
    for i in range(SAMPLES):
        raw = raw_s[3, i]
        spacing = gap_s[i]
        tau = softplus(raw) * spacing
        depth = depth + tau
        share.append(through * (1.0 - jnp.exp(-tau)))
        through = jnp.exp(-depth)
        clear.append(through)
        spans.append(spacing)
        color = [color[c] + share[i] * shade[c][i] for c in range(3)]

    turn[0:16, :] = jnp.concatenate(color + [through], axis=0)
    flipped = turn[...].T
    table_t[...] = flipped
    row_b = jnp.zeros((n_vol, 128), F32)
    for j in range(CAP):
        piece = table_t[pl.ds(j, n_vol, stride=CAP), :]
        row_b = row_b + (piece if j == 0 else pltpu.roll(piece, 16 * j, 1))
    send_b[...] = row_b.reshape(n_vol, 1, 128)
    recv_b[me_v] = send_b[me_v]
    exchange(send_b, recv_b, 1)

    dense_slope = [spans[i] * sigmoid(raw_s[3, i]) for i in range(SAMPLES)]
    color_slope = [
        [share[i] * (shade[c][i] * (1.0 - shade[c][i])) for i in range(SAMPLES)] for c in range(3)
    ]

    def slopes(v, carry):
        for i in range(SAMPLES):
            span = slice(i * lanes, (i + 1) * lanes)
            for w_t, before_s, after_s, slope_s in (
                (w_in_t, enc, act_one, slope_one),
                (w_hidden_t, act_one, act_two, slope_two),
            ):
                half = dot(w_t[v], before_s[v, :, span])
                turned = jnp.tanh(half)
                slope_s[v, :, span] = 0.5 * (1.0 + turned + half * (1.0 - turned * turned))
        return carry

    owner_hot = one_hot(n_vol, owner).astype(BF16)
    spot = lax.broadcasted_iota(jnp.int32, (128, segs), 0)
    mine = jnp.where(lax.bitwise_and(spot, 0x73) == rank * 16 + held, 1.0, 0.0)
    mine_s[...] = mine
    lax.fori_loop(0, HELD // 2, slopes, 0)
    await_all(recv_b, 3)

    mine = mine_s[...]
    arrived = recv_b[...].reshape(n_vol, 128)
    arrived = jnp.concatenate([arrived, jnp.zeros((128 - n_vol, 128), F32)], axis=0)
    arrived_t = arrived.T[:, 0:n_vol]
    found = dot(split3(arrived_t, 1), jnp.concatenate([owner_hot] * 3, axis=0))
    found = found * mine
    total = found[0:16]
    for j in range(1, CAP):
        total = total + found[16 * j : 16 * j + 16]
    per_seg = [jnp.sum(total[4 * c : 4 * c + 4], axis=0, keepdims=True) for c in range(4)]
    carried = per_seg[3][:, :rays]
    behind = jnp.zeros((1, rays), F32)
    cots = []
    for c in range(3):
        near, far = per_seg[c][:, :rays], per_seg[c][:, rays:]
        value = near + carried * far
        out_color[c : c + 1, :] = value
        slope = (value - target[c : c + 1, :]) * (1.0 / n_rep)
        behind = behind + slope * far
        cots.append(jnp.concatenate([slope, carried * slope], axis=1))
    cots.append(jnp.concatenate([behind, jnp.zeros((1, rays), F32)], axis=1))
    cots = jnp.concatenate([jnp.broadcast_to(x, (4, segs)) for x in cots], axis=0)
    cots = jnp.concatenate([cots] * CAP, axis=0) * mine
    row_c = dot_nt(owner_hot, split3(cots, 0))
    row_c = (row_c[:, 0:128] + row_c[:, 128:256]) + row_c[:, 256:384]
    send_c[...] = row_c.reshape(n_vol, 1, 128)
    recv_c[me_v] = send_c[me_v]
    exchange(send_c, recv_c, 2)

    lax.fori_loop(HELD // 2, HELD, slopes, 0)
    await_all(recv_c, 5)

    row_c = recv_c[...].reshape(n_vol, 128)
    for j in range(CAP):
        piece = row_c if j == 0 else pltpu.roll(row_c, 128 - 16 * j, 1)
        table_t[pl.ds(j, n_vol, stride=CAP), :] = piece
    cots = table_t[...].T[0:16]
    cot_color = [cots[4 * c : 4 * c + 4] for c in range(3)]
    later = through * cots[12:16]
    for i in reversed(range(SAMPLES)):
        pull = sum(cot_color[c] * shade[c][i] for c in range(3))
        cot_raw = [cot_color[c] * color_slope[c][i] for c in range(3)]
        cot_raw.append((clear[i] * pull - later) * dense_slope[i])
        later = later + share[i] * pull
        for c in range(4):
            for v in range(HELD):
                cot_f[v, c : c + 1, i * lanes : (i + 1) * lanes] = cot_raw[c][v : v + 1]

    def pair_copy(v):
        return pltpu.make_async_remote_copy(
            src_ref=part.at[v, 1 - me_c],
            dst_ref=pair_in.at[v],
            send_sem=pair_sem.at[0, v],
            recv_sem=pair_sem.at[1, v],
            device_id=(sibling, me_v),
            device_id_type=MESH,
        )

    def pass_on(v):
        pair_copy(v).wait()
        both = part[v, me_c] + pair_in[v]
        block_out[v] = both.astype(BF16)
        own_block[...] = both
        pair_in[v, 0] = own_block[me_y]
        block_in[v, me_y] = jnp.zeros((rows, PACK), BF16)

        for y in y_peers:
            pltpu.make_async_remote_copy(
                src_ref=block_out.at[v, y],
                dst_ref=block_in.at[v, me_y],
                send_sem=block_sem.at[0, v],
                recv_sem=block_sem.at[1, v],
                device_id=(y * 2 + me_c, me_v),
                device_id_type=MESH,
            ).start()

    def backward(v, carry):
        for i in range(SAMPLES):
            span = slice(i * lanes, (i + 1) * lanes)
            cot_raw = cot_f[v, 0:4, span].astype(BF16).astype(F32)
            cot = sum(
                cot_raw[c : c + 1] * jnp.concatenate([w_head_w[v, c]] * blocks, axis=1)
                for c in range(4)
            )
            cot = cot * slope_two[v, :, span]
            cot = cot.astype(BF16)
            cot_two_s[:, span] = cot
            cot = dot(w_hidden[v], cot) * slope_one[v, :, span]
            cot_one_s[:, span] = cot.astype(BF16)
        d_mid = dot_nt(act_one[v], cot_two_s[...])
        d_first = dot_nt(cot_one_s[...], enc[v])
        d_last = dot_nt(cot_f[v].astype(BF16), act_two[v])
        d_last = jnp.concatenate([d_last, jnp.zeros((112, WIDTH), F32)], axis=0).T[:, 0:64]
        side = jnp.concatenate([d_first, d_last], axis=1)
        for r in range(n_rep):
            part[v, r % 2, r // 2, :, 0:WIDTH] = d_mid[r * rows : (r + 1) * rows]
            part[v, r % 2, r // 2, :, WIDTH:PACK] = side[r * rows : (r + 1) * rows]
        pair_copy(v).start()

        @pl.when(v > 0)
        def _():
            pass_on(v - 1)

        return carry

    lax.fori_loop(0, HELD, backward, 0)
    pass_on(HELD - 1)

    heads = []
    for v in range(HELD):
        span = block_in.at[v, pl.ds(0, n_y - 1)]
        pltpu.make_async_copy(span, span, block_sem.at[1, v]).wait()
        whole = pair_in[v, 0]
        for y in range(n_y):
            whole = whole + block_in[v, y].astype(F32)
        out_hidden[v] = whole[:, 0:WIDTH]
        out_in[v] = whole[:, WIDTH : WIDTH + ENC]
        heads.append(whole[:, WIDTH:PACK])
    heads.append(jnp.zeros((max(128 - HELD * rows, 0), 128), F32))
    heads = jnp.concatenate(heads, axis=0).T
    for v in range(HELD):
        out_head[v] = heads[ENC : ENC + 4, v * rows : (v + 1) * rows]

    for number, buffer in ((0, send_a), (1, send_b), (2, send_c)):
        await_all(buffer, 2 * number)
    for v in range(HELD):
        span = block_out.at[v, pl.ds(0, n_y - 1)]
        pltpu.make_async_copy(span, span, block_sem.at[0, v]).wait()


def hand_over(*refs):
    for source, result in zip(refs[:4], refs[4:]):
        result[...] = source[...]


def solution(mesh):
    n_rep, n_vol = mesh.shape["rep"], mesh.shape["vol"]

    def local(positions, spacing, volume_ids, target, w_in, w_hidden, w_head):
        rays = volume_ids.shape[0]
        lanes = n_vol * CAP
        wide = SAMPLES * lanes
        rows = WIDTH // n_rep
        n_y = n_rep // 2
        vmem = pl.BlockSpec(memory_space=pltpu.VMEM)
        shapes = (
            jax.ShapeDtypeStruct((3, rays), F32),
            jax.ShapeDtypeStruct((HELD, rows, ENC), F32),
            jax.ShapeDtypeStruct((HELD, rows, WIDTH), F32),
            jax.ShapeDtypeStruct((HELD, 4, rows), F32),
        )
        outs = pl.pallas_call(
            functools.partial(kernel, n_rep, n_vol, rays),
            out_shape=shapes,
            in_specs=[pl.BlockSpec(memory_space=pl.ANY)] * 7,
            out_specs=[vmem] * 4,
            scratch_shapes=[
                pltpu.VMEM((n_vol, CAP, 128), F32),
                pltpu.VMEM((n_vol, CAP, 128), F32),
                pltpu.VMEM((n_vol, 1, 128), F32),
                pltpu.VMEM((n_vol, 1, 128), F32),
                pltpu.VMEM((n_vol, 1, 128), F32),
                pltpu.VMEM((n_vol, 1, 128), F32),
                pltpu.VMEM((128, lanes), F32),
                pltpu.VMEM((pl.cdiv(lanes, 128), ENC * 8, min(lanes, 128)), F32),
                pltpu.VMEM((HELD, ENC, wide), BF16),
                pltpu.VMEM((HELD, WIDTH, wide), BF16),
                pltpu.VMEM((HELD, WIDTH, wide), BF16),
                pltpu.VMEM((HELD, WIDTH, wide), F32),
                pltpu.VMEM((HELD, WIDTH, wide), F32),
                pltpu.VMEM((128, 2 * rays), F32),
                pltpu.VMEM((4, SAMPLES, HELD, lanes), F32),
                pltpu.VMEM((SAMPLES, HELD, lanes), F32),
                pltpu.VMEM((HELD, 16, wide), F32),
                pltpu.VMEM((WIDTH, wide), BF16),
                pltpu.VMEM((WIDTH, wide), BF16),
                pltpu.VMEM((128, lanes), F32),
                pltpu.VMEM((lanes, 128), F32),
                pltpu.VMEM((HELD, WIDTH, ENC), BF16),
                pltpu.VMEM((HELD, WIDTH, WIDTH), BF16),
                pltpu.VMEM((HELD, 16, WIDTH), BF16),
                pltpu.VMEM((HELD, 4, WIDTH, min(lanes, 128)), F32),
                pltpu.VMEM((HELD, 2, n_y, rows, PACK), F32),
                pltpu.VMEM((HELD, n_y, rows, PACK), F32),
                pltpu.VMEM((HELD, n_y, rows, PACK), BF16),
                pltpu.VMEM((HELD, n_y, rows, PACK), BF16),
                pltpu.VMEM((n_y, rows, PACK), F32),
                pltpu.VMEM((2, 3 * SAMPLES, rays), F32),
                pltpu.VMEM((2, SAMPLES, rays), F32),
                pltpu.VMEM((2, rays), jnp.int32),
                pltpu.VMEM((3, rays), F32),
                pltpu.VMEM(w_in.shape, BF16),
                pltpu.VMEM(w_hidden.shape, BF16),
                pltpu.VMEM(w_head.shape, BF16),
                pltpu.SemaphoreType.DMA((6,)),
                pltpu.SemaphoreType.DMA((2, HELD)),
                pltpu.SemaphoreType.DMA((2, HELD)),
                pltpu.SemaphoreType.DMA((7,)),
            ],
            compiler_params=pltpu.CompilerParams(
                collective_id=0, has_side_effects=True, vmem_limit_bytes=56 * 1024 * 1024
            ),
        )(
            jnp.transpose(positions, (1, 2, 0)),
            jnp.transpose(spacing, (1, 2, 0)),
            volume_ids.T,
            target,
            w_in,
            w_hidden,
            w_head,
        )
        color, grad_in, grad_hidden, grad_head = pl.pallas_call(
            hand_over, out_shape=shapes, in_specs=[vmem] * 4, out_specs=[vmem] * 4
        )(*outs)
        return color, jnp.swapaxes(grad_in, 1, 2), grad_hidden, grad_head

    return jax.shard_map(
        local,
        mesh=mesh,
        in_specs=(
            P(("rep", "vol"), None, None),
            P(("rep", "vol"), None, None),
            P(("rep", "vol"), None),
            P(None, ("rep", "vol")),
            P("vol", None, None),
            P("vol", None, None),
            P("vol", None, None),
        ),
        out_specs=(
            P(None, ("rep", "vol")),
            P("vol", None, "rep"),
            P("vol", "rep", None),
            P("vol", None, "rep"),
        ),
        check_vma=False,
    )
```
